512 devices in a mesh: cand: 32 (over x_lo, y, core), ref: 16 (over z, x_hi).
Axes of the slice: x: 4 (x_hi: 2, x_lo: 2; x = x_hi * 2 + x_lo), y: 8, z: 8, core: 2. Of those that a mesh axis runs over, the one named last changes fastest.
Arguments:
- cand_factor: float32 [32768, 512], P('cand'), may hold values from -6 to 6
- ref_factor: float32 [8192, 512], P('ref'), may hold values from -6 to 6
- cand_plan: float32 [32768, 128], P('cand'), may hold values from 0.0625 to 16
- ref_plan: float32 [8192, 128], P('ref'), may hold values from 0.0625 to 16
- weights: float32 [128], replicated, may hold values from 0.5 to 2
Outputs:
- new_cand_plan: float32 [32768, 128], P('cand')
- new_ref_plan: float32 [8192, 128], P('ref')
- new_weights: float32 [128], replicated
The draws below stay inside these ranges and needn't reach their ends.
All inputs are finite; a program needn't handle non-finite values. Where the reference program divides by a largest or mean magnitude, that divisor is 1e-20 or more.
Results may differ from the reference program's by a relative error of at most 0.00019.
Values sent between devices are 32-bit elements; how exact they have to be, the bound alone decides.
A program may use at most 64 MiB of HBM per device.

```python
import math
import jax
import jax.numpy as jnp
from jax import lax

D = 512
RK = 128
ITERS = 3
NQ = 32768
NR = 8192


def offset_factor(key, row_count, with_offset):
    noise = jax.random.normal(jax.random.fold_in(key, 201), (row_count, D), jnp.float32)
    if with_offset:
        shared = 0.5 * jax.random.normal(jax.random.fold_in(key, 202), (D,), jnp.float32)
        noise = noise + shared[None, :]
    return jnp.clip(noise, -6.0, 6.0)


def column_blocks(key):
    return jax.random.permutation(jax.random.fold_in(key, 101), RK) % 4


def block_plan(key, row_count, salt):
    col_block = column_blocks(key)
    counts = jax.random.randint(jax.random.fold_in(key, salt), (4,), 1, 5)
    picks = jax.random.randint(jax.random.fold_in(key, salt + 1), (row_count,), 0, jnp.sum(counts))
    bounds = jnp.cumsum(counts)
    row_block = jnp.sum((picks[:, None] >= bounds[None, :]).astype(jnp.int32), axis=1)
    base = jnp.exp(jax.random.uniform(jax.random.fold_in(key, salt + 2), (row_count, RK), jnp.float32, math.log(0.25), math.log(4.0)))
    boost = jnp.where(row_block[:, None] == col_block[None, :], 4.0, 0.25)
    return (base * boost).astype(jnp.float32)


def draw_cand_factor(key, part):
    return offset_factor(key, NQ, True)


def draw_ref_factor(key, part):
    return offset_factor(jax.random.fold_in(key, 7), NR, False)


def draw_cand_plan(key, part):
    return block_plan(key, NQ, 300)


def draw_ref_plan(key, part):
    return block_plan(key, NR, 400)


def setup_inputs(seed: int = 0) -> dict:
    key_of = jax.random.split(jax.random.key(seed), 6)
    cand_factor = draw_cand_factor(jax.random.fold_in(key_of[5], 71), 0)
    ref_factor = draw_ref_factor(jax.random.fold_in(key_of[5], 71), 0)
    cand_plan = draw_cand_plan(jax.random.fold_in(key_of[5], 71), 0)
    ref_plan = draw_ref_plan(jax.random.fold_in(key_of[5], 71), 0)
    weights = jnp.clip(jnp.exp(jax.random.uniform(key_of[4], (RK,), jnp.float32, math.log(0.5), math.log(2.0))), 0.5, 2.0)
    return {"cand_factor": cand_factor, "ref_factor": ref_factor, "cand_plan": cand_plan, "ref_plan": ref_plan, "weights": weights}


step_size = 3.0
tiny_value = 1e-6


def contract_rows(left, right):
    return lax.dot_general(left, right, (((0,), (0,)), ((), ())), precision=lax.Precision.HIGHEST, preferred_element_type=jnp.float32)


def reference(cand_factor, ref_factor, cand_plan, ref_plan, weights):
    cand_moment = contract_rows(cand_factor, cand_plan) / NQ
    ref_moment = contract_rows(ref_factor, ref_plan) / NR
    grad_cand = jnp.dot(cand_factor, ref_moment, precision=lax.Precision.HIGHEST) / weights[None, :]
    grad_ref = jnp.dot(ref_factor, cand_moment, precision=lax.Precision.HIGHEST) / weights[None, :]
    grad_weights = -jnp.sum(cand_moment * ref_moment, axis=0) / (weights * weights)
    top = jnp.maximum(jnp.maximum(jnp.max(jnp.abs(grad_cand)), jnp.max(jnp.abs(grad_ref))), jnp.max(jnp.abs(grad_weights))) + tiny_value
    kernel_cand = cand_plan * jnp.exp(-step_size * grad_cand / top)
    kernel_ref = ref_plan * jnp.exp(-step_size * grad_ref / top)
    kernel_weights = weights * jnp.exp(-step_size * grad_weights / top)
    scale_cand = jnp.ones((RK,), jnp.float32)
    scale_ref = jnp.ones((RK,), jnp.float32)
    for repeat_index in range(ITERS):
        row_cand = RK / jnp.dot(kernel_cand, scale_cand, precision=lax.Precision.HIGHEST)
        row_ref = RK / jnp.dot(kernel_ref, scale_ref, precision=lax.Precision.HIGHEST)
        mass_cand = jnp.dot(row_cand, kernel_cand, precision=lax.Precision.HIGHEST) / NQ
        mass_ref = jnp.dot(row_ref, kernel_ref, precision=lax.Precision.HIGHEST) / NR
        new_weights = jnp.cbrt(kernel_weights * scale_cand * mass_cand * scale_ref * mass_ref)
        scale_cand = new_weights / mass_cand
        scale_ref = new_weights / mass_ref
    new_cand_plan = row_cand[:, None] * kernel_cand * scale_cand[None, :]
    new_ref_plan = row_ref[:, None] * kernel_ref * scale_ref[None, :]
    return new_cand_plan, new_ref_plan, new_weights
```

```python
import functools

import jax
import jax.numpy as jnp
from jax import lax
from jax.experimental import pallas as pl
from jax.experimental.pallas import tpu as pltpu
from jax.sharding import PartitionSpec as P

ITERS = 3
STEP_SIZE = 3.0
TINY = 1e-06
LANES = 128
MESH = pl.DeviceIdType.MESH
F32 = jnp.float32
BF16 = jnp.bfloat16


def contract_rows(left, right):
    return lax.dot_general(
        left,
        right,
        (((0,), (0,)), ((), ())),
        precision=lax.Precision.HIGHEST,
        preferred_element_type=F32,
    )


def split(x):
    high = x.astype(BF16)
    return high, (x - high.astype(F32)).astype(BF16)


def cube_root(x):
    y = jnp.exp(jnp.log(x) * (1.0 / 3.0))
    return y - (y * y * y - x) / (3.0 * y * y)


def wait_bytes(ref, sem):
    pltpu.make_async_copy(ref, ref, sem).wait()


def kernel(
    n_cand,
    n_ref,
    cand_factor,
    ref_factor,
    cand_plan,
    ref_plan,
    weights,
    new_cand_plan,
    new_ref_plan,
    new_weights_out,
    cf,
    rf,
    cf_block,
    rf_block,
    cp,
    rp,
    cf_high,
    cf_low,
    rf_high,
    rf_low,
    kc,
    kr,
    moment_c,
    moment_r,
    part_c,
    part_r,
    rs_c,
    rs_r,
    ag_c,
    ag_r,
    cand_moment,
    ref_moment,
    out_row,
    in_c,
    in_r,
    load_sems,
    store_sems,
    send_c,
    send_r,
    recv_c,
    recv_r,
):
    c = lax.axis_index("cand")
    r = lax.axis_index("ref")
    rows_c, depth = cf.shape
    rows_r = rf.shape[0]
    width_c = depth // n_ref
    width_r = depth // n_cand
    own = depth // (n_cand * n_ref)

    barrier = pltpu.get_barrier_semaphore()

    def greet_c(i, _):
        pl.semaphore_signal(
            barrier, inc=1, device_id=(lax.rem(c + i, n_cand), r), device_id_type=MESH
        )
        return 0

    def greet_r(i, _):
        pl.semaphore_signal(
            barrier, inc=1, device_id=(c, lax.rem(r + i, n_ref)), device_id_type=MESH
        )
        return 0

    group_c = (r * width_c) // LANES
    group_r = (c * width_r) // LANES
    loads = [
        pltpu.make_async_copy(
            cand_factor.at[:, pl.ds(pl.multiple_of(group_c * LANES, LANES), LANES)],
            cf_block,
            load_sems.at[0],
        ),
        pltpu.make_async_copy(cand_plan, cp, load_sems.at[1]),
        pltpu.make_async_copy(
            ref_factor.at[:, pl.ds(pl.multiple_of(group_r * LANES, LANES), LANES)],
            rf_block,
            load_sems.at[2],
        ),
        pltpu.make_async_copy(ref_plan, rp, load_sems.at[3]),
        pltpu.make_async_copy(cand_factor, cf, load_sems.at[4]),
        pltpu.make_async_copy(ref_factor, rf, load_sems.at[5]),
    ]
    for load in loads:
        load.start()
    lax.fori_loop(1, n_cand, greet_c, 0)
    lax.fori_loop(1, n_ref, greet_r, 0)

    def send_to_c(phase, source, target):
        def body(i, _):
            peer = lax.rem(c + i, n_cand)
            pltpu.make_async_remote_copy(
                src_ref=source(peer),
                dst_ref=target(c),
                send_sem=send_c.at[phase],
                recv_sem=recv_c.at[phase],
                device_id=(peer, r),
                device_id_type=MESH,
            ).start()
            return 0

        lax.fori_loop(1, n_cand, body, 0)

    def send_to_r(phase, source, target):
        def body(i, _):
            peer = lax.rem(r + i, n_ref)
            pltpu.make_async_remote_copy(
                src_ref=source(peer),
                dst_ref=target(r),
                send_sem=send_r.at[phase],
                recv_sem=recv_r.at[phase],
                device_id=(c, peer),
                device_id_type=MESH,
            ).start()
            return 0

        lax.fori_loop(1, n_ref, body, 0)

    loads[0].wait()
    loads[1].wait()
    moment_c[...] = contract_rows(cf_block[...], cp[...]) * (1.0 / (rows_c * n_cand))
    sub_c = pl.multiple_of(r * width_c - group_c * LANES, width_c)
    part_c[...] = moment_c[pl.ds(sub_c, width_c), :].reshape(part_c.shape)
    loads[2].wait()
    loads[3].wait()
    moment_r[...] = contract_rows(rf_block[...], rp[...]) * (1.0 / (rows_r * n_ref))
    sub_r = pl.multiple_of(c * width_r - group_r * LANES, width_r)
    part_r[...] = moment_r[pl.ds(sub_r, width_r), :].reshape(part_r.shape)

    pl.semaphore_wait(barrier, n_cand + n_ref - 2)

    send_to_c(0, lambda peer: part_c.at[peer], lambda me: rs_c.at[me])
    send_to_r(0, lambda peer: part_r.at[peer], lambda me: rs_r.at[me])
    rs_c[c] = part_c[c]
    rs_r[r] = part_r[r]

    loads[4].wait()
    tile = min(rows_c, 64)

    @pl.loop(0, rows_c, step=tile)
    def _(at):
        at = pl.multiple_of(at, tile)
        high, low = split(cf[pl.ds(at, tile), :])
        cf_high[pl.ds(at, tile), :] = high
        cf_low[pl.ds(at, tile), :] = low

    wait_bytes(rs_c.at[pl.ds(0, n_cand - 1)], recv_c.at[0])
    ag_c[c] = jnp.sum(rs_c[...], axis=0)
    send_to_c(1, lambda peer: ag_c.at[c], lambda me: ag_c.at[me])
    wait_bytes(rs_r.at[pl.ds(0, n_ref - 1)], recv_r.at[0])
    ag_r[r] = jnp.sum(rs_r[...], axis=0)
    send_to_r(1, lambda peer: ag_r.at[r], lambda me: ag_r.at[me])

    loads[5].wait()

    @pl.loop(0, rows_r, step=tile)
    def _(at):
        at = pl.multiple_of(at, tile)
        high, low = split(rf[pl.ds(at, tile), :])
        rf_high[pl.ds(at, tile), :] = high
        rf_low[pl.ds(at, tile), :] = low

    def place_c(who):
        return cand_moment.at[pl.ds(pl.multiple_of(who * width_c, width_c), width_c)]

    def place_r(who):
        return ref_moment.at[pl.ds(pl.multiple_of(who * width_r, width_r), width_r)]

    wait_bytes(ag_c.at[pl.ds(0, n_cand - 1)], recv_c.at[1])
    place_c(r)[...] = ag_c[...].reshape(width_c, LANES)
    send_to_r(2, lambda peer: place_c(r), place_c)
    wait_bytes(ag_r.at[pl.ds(0, n_ref - 1)], recv_r.at[1])
    place_r(c)[...] = ag_r[...].reshape(width_r, LANES)
    send_to_c(2, lambda peer: place_r(c), place_r)

    weights_row = weights[...]
    weights_inverse = 1.0 / weights_row

    def gradient(high, low, moment, out, rows):
        right = jnp.concatenate(split(moment[...]), axis=1)
        step = min(rows, 256)

        def body(i, top):
            at = pl.multiple_of(i * step, step)
            both = jnp.dot(
                high[pl.ds(at, step), :], right, preferred_element_type=F32
            ) + jnp.dot(low[pl.ds(at, step), :], right, preferred_element_type=F32)
            grad = (both[:, :LANES] + both[:, LANES:]) * weights_inverse
            out[pl.ds(at, step), :] = grad
            return jnp.maximum(top, jnp.max(jnp.abs(grad), axis=0, keepdims=True))

        return lax.fori_loop(0, rows // step, body, jnp.zeros((1, LANES), F32))

    wait_bytes(ref_moment.at[pl.ds(0, depth - width_r)], recv_c.at[2])
    top_c = gradient(cf_high, cf_low, ref_moment, kc, rows_c)
    wait_bytes(cand_moment.at[pl.ds(0, depth - width_c)], recv_r.at[2])
    top_r = gradient(rf_high, rf_low, cand_moment, kr, rows_r)

    def exchange(phase, row_c, row_r):
        slot = phase - 3
        out_row[slot, 0] = row_c
        out_row[slot, 1] = row_r
        send_to_c(
            phase, lambda peer: out_row.at[slot, 0], lambda me: in_c.at[slot, me]
        )
        send_to_r(
            phase, lambda peer: out_row.at[slot, 1], lambda me: in_r.at[slot, me]
        )
        in_c[slot, c] = row_c
        in_r[slot, r] = row_r
        wait_bytes(in_c.at[slot, pl.ds(0, n_cand - 1)], recv_c.at[phase])
        wait_bytes(in_r.at[slot, pl.ds(0, n_ref - 1)], recv_r.at[phase])
        return in_c[slot], in_r[slot]

    local = jnp.maximum(top_c, top_r)
    tops_c, tops_r = exchange(3, local, local)
    grad_weights = -jnp.sum(
        cand_moment[...] * ref_moment[...], axis=0, keepdims=True
    ) / (weights_row * weights_row)
    tops = jnp.maximum(jnp.max(tops_c, axis=0), jnp.max(tops_r, axis=0))
    tops = jnp.maximum(tops, jnp.abs(grad_weights))
    top = jnp.max(tops, axis=1, keepdims=True) + TINY
    factor = -STEP_SIZE / top
    kernel_weights = weights_row * jnp.exp(grad_weights * factor)

    scale_c = jnp.ones((1, LANES), F32)
    scale_r = jnp.ones((1, LANES), F32)

    def row_pass(k, plan, scale, rows, first, last):
        step = min(rows, 128)

        def body(i, mass):
            at = pl.multiple_of(i * step, step)
            here = pl.ds(at, step)
            if first:
                block = plan[here, :] * jnp.exp(k[here, :] * factor)
                k[here, :] = block
                total = jnp.sum(block, axis=1, keepdims=True)
            else:
                block = k[here, :]
                total = jnp.sum(block * scale, axis=1, keepdims=True)
            scaled = block * (LANES / total)
            if last:
                k[here, :] = scaled
            return mass + jnp.sum(scaled.reshape(step // 8, 8, LANES), axis=0)

        mass = lax.fori_loop(0, rows // step, body, jnp.zeros((8, LANES), F32))
        return jnp.sum(mass, axis=0, keepdims=True)

    for i in range(ITERS):
        first, last = i == 0, i == ITERS - 1
        part_mass_c = row_pass(kc, cp, scale_c, rows_c, first, last)
        part_mass_r = row_pass(kr, rp, scale_r, rows_r, first, last)
        masses_c, masses_r = exchange(4 + i, part_mass_c, part_mass_r)
        mass_c = jnp.sum(masses_c, axis=0) * (1.0 / (rows_c * n_cand))
        mass_r = jnp.sum(masses_r, axis=0) * (1.0 / (rows_r * n_ref))
        new_weights = cube_root(kernel_weights * scale_c * mass_c * scale_r * mass_r)
        scale_c = new_weights / mass_c
        scale_r = new_weights / mass_r

    kc[...] = kc[...] * scale_c
    store_c = pltpu.make_async_copy(kc, new_cand_plan, store_sems.at[0])
    store_c.start()
    kr[...] = kr[...] * scale_r
    store_r = pltpu.make_async_copy(kr, new_ref_plan, store_sems.at[1])
    store_r.start()
    new_weights_out[...] = new_weights

    wait_bytes(part_c.at[pl.ds(0, n_cand - 1)], send_c.at[0])
    wait_bytes(part_r.at[pl.ds(0, n_ref - 1)], send_r.at[0])
    wait_bytes(ag_c.at[pl.ds(0, n_cand - 1)], send_c.at[1])
    wait_bytes(ag_r.at[pl.ds(0, n_ref - 1)], send_r.at[1])
    wait_bytes(cand_moment.at[pl.ds(0, depth - width_c)], send_r.at[2])
    wait_bytes(ref_moment.at[pl.ds(0, depth - width_r)], send_c.at[2])
    for slot in range(1 + ITERS):
        wait_bytes(in_c.at[slot, pl.ds(0, n_cand - 1)], send_c.at[3 + slot])
        wait_bytes(in_r.at[slot, pl.ds(0, n_ref - 1)], send_r.at[3 + slot])
    store_c.wait()
    store_r.wait()


def on_device(n_cand, n_ref, cand_factor, ref_factor, cand_plan, ref_plan, weights):
    rows_c, depth = cand_factor.shape
    rows_r = ref_factor.shape[0]
    rank = weights.shape[0]
    width_c, width_r = depth // n_ref, depth // n_cand
    own = depth // (n_cand * n_ref)
    phases = 4 + ITERS
    anywhere = pl.BlockSpec(memory_space=pl.ANY)
    vmem = pl.BlockSpec(memory_space=pltpu.VMEM)
    new_cand_plan, new_ref_plan, new_weights = pl.pallas_call(
        functools.partial(kernel, n_cand, n_ref),
        out_shape=(
            jax.ShapeDtypeStruct((rows_c, rank), F32),
            jax.ShapeDtypeStruct((rows_r, rank), F32),
            jax.ShapeDtypeStruct((1, rank), F32),
        ),
        in_specs=[anywhere] * 4 + [vmem],
        out_specs=(anywhere, anywhere, vmem),
        scratch_shapes=[
            pltpu.VMEM((rows_c, depth), F32),
            pltpu.VMEM((rows_r, depth), F32),
            pltpu.VMEM((rows_c, LANES), F32),
            pltpu.VMEM((rows_r, LANES), F32),
            pltpu.VMEM((rows_c, rank), F32),
            pltpu.VMEM((rows_r, rank), F32),
            pltpu.VMEM((rows_c, depth), BF16),
            pltpu.VMEM((rows_c, depth), BF16),
            pltpu.VMEM((rows_r, depth), BF16),
            pltpu.VMEM((rows_r, depth), BF16),
            pltpu.VMEM((rows_c, rank), F32),
            pltpu.VMEM((rows_r, rank), F32),
            pltpu.VMEM((LANES, rank), F32),
            pltpu.VMEM((LANES, rank), F32),
            pltpu.VMEM((n_cand, own, rank), F32),
            pltpu.VMEM((n_ref, own, rank), F32),
            pltpu.VMEM((n_cand, own, rank), F32),
            pltpu.VMEM((n_ref, own, rank), F32),
            pltpu.VMEM((n_cand, own, rank), F32),
            pltpu.VMEM((n_ref, own, rank), F32),
            pltpu.VMEM((depth, rank), F32),
            pltpu.VMEM((depth, rank), F32),
            pltpu.VMEM((1 + ITERS, 2, 1, rank), F32),
            pltpu.VMEM((1 + ITERS, n_cand, 1, rank), F32),
            pltpu.VMEM((1 + ITERS, n_ref, 1, rank), F32),
            pltpu.SemaphoreType.DMA((6,)),
            pltpu.SemaphoreType.DMA((2,)),
            pltpu.SemaphoreType.DMA((phases,)),
            pltpu.SemaphoreType.DMA((phases,)),
            pltpu.SemaphoreType.DMA((phases,)),
            pltpu.SemaphoreType.DMA((phases,)),
        ],
        compiler_params=pltpu.CompilerParams(
            collective_id=0, has_side_effects=True, vmem_limit_bytes=32 * 2**20
        ),
    )(cand_factor, ref_factor, cand_plan, ref_plan, weights.reshape(1, rank))
    return new_cand_plan, new_ref_plan, new_weights.reshape(rank)


def solution(mesh):
    in_specs = (P("cand", None), P("ref", None), P("cand", None), P("ref", None), P())
    out_specs = (P("cand", None), P("ref", None), P())
    return jax.shard_map(
        functools.partial(on_device, mesh.shape["cand"], mesh.shape["ref"]),
        mesh=mesh,
        in_specs=in_specs,
        out_specs=out_specs,
        check_vma=False,
    )
```

```python
import functools

import jax
import jax.numpy as jnp
from jax import lax
from jax.experimental import pallas as pl
from jax.experimental.pallas import tpu as pltpu
from jax.sharding import PartitionSpec as P

ITERS = 3
STEP_SIZE = 3.0
TINY = 1e-06
LANES = 128
MESH = pl.DeviceIdType.MESH
F32 = jnp.float32
BF16 = jnp.bfloat16


def split(x):
    high = x.astype(BF16)
    return high, (x - high.astype(F32)).astype(BF16)


def contract_rows(left, right):
    both = lax.dot_general(
        jnp.concatenate(split(left), axis=1),
        jnp.concatenate(split(right), axis=1),
        (((0,), (0,)), ((), ())),
        preferred_element_type=F32,
    )
    half = left.shape[1]
    return (both[:half, :LANES] + both[half:, LANES:]) + (
        both[half:, :LANES] + both[:half, LANES:]
    )


def cube_root(x):
    y = jnp.exp(jnp.log(x) * (1.0 / 3.0))
    return y - (y * y * y - x) / (3.0 * y * y)


def wait_bytes(ref, sem):
    pltpu.make_async_copy(ref, ref, sem).wait()


def kernel(
    n_cand,
    n_ref,
    cand_factor,
    ref_factor,
    cand_plan,
    ref_plan,
    weights_in,
    scaled_cand,
    scaled_ref,
    rows_out,
    cf,
    rf,
    cf_block,
    rf_block,
    cp,
    rp,
    weights,
    cf_high,
    cf_low,
    rf_high,
    rf_low,
    kc,
    kr,
    moment_c,
    moment_r,
    part_c,
    pair_c,
    sum_c,
    sum_r,
    cand_moment,
    ref_moment,
    out_row,
    in_c,
    in_r,
    load_sems,
    store_sems,
    pair_send,
    pair_recv,
    send_c,
    send_r,
    recv_c,
    recv_r,
):
    c = lax.axis_index("cand")
    r = lax.axis_index("ref")
    n_y, n_z = n_cand // 4, n_ref // 2
    core = lax.rem(c, 2)
    y = lax.rem(c // 2, n_y)
    x_lo = c // (2 * n_y)
    x_hi = lax.rem(r, 2)
    z = r // 2
    spot = x_lo * n_y + y
    side = lax.rem(x_lo + x_hi, 2)
    rows_c, depth = cf.shape
    rows_r = rf.shape[0]
    width_c = depth // n_ref
    width_r = depth // n_cand
    part = width_c // 2
    sibling = 1 - core

    def away(step, size):
        turn = lax.rem(step, 2) * 2 - 1
        return lax.rem(size // 2 + turn * ((step + 1) // 2) + size, size)

    def to_c(flip, offset_y, flip_core):
        new_x = lax.rem(x_lo + flip, 2)
        new_core = lax.rem(core + flip_core, 2)
        return ((new_x * n_y + lax.rem(y + offset_y, n_y)) * 2 + new_core, r)

    def to_r(flip, offset_z):
        new_c = (lax.rem(x_lo + flip, 2) * n_y + y) * 2 + core
        return (new_c, lax.rem(z + offset_z, n_z) * 2 + lax.rem(x_hi + flip, 2))

    def for_all(visit_c, visit_r, cores):
        def body(step, _):
            offset_y = away(step, n_y)
            for flip in (1, 0):
                for flip_core in cores:
                    visit_c(to_c(flip, offset_y, flip_core))
            if n_z == n_y:
                for flip in (1, 0):
                    visit_r(to_r(flip, offset_y))
            return 0

        lax.fori_loop(0, n_y - 1, body, 0)
        if n_z != n_y:

            def body_r(step, _):
                for flip in (1, 0):
                    visit_r(to_r(flip, away(step, n_z)))
                return 0

            lax.fori_loop(0, n_z - 1, body_r, 0)
        for flip_core in cores:
            visit_c(to_c(1, 0, flip_core))
        visit_r(to_r(1, 0))
        if 1 in cores:
            visit_c(to_c(0, 0, 1))

    barrier = pltpu.get_barrier_semaphore()

    def greet(device):
        pl.semaphore_signal(barrier, inc=1, device_id=device, device_id_type=MESH)

    def remote(source, target, send, recv, device):
        return pltpu.make_async_remote_copy(
            src_ref=source,
            dst_ref=target,
            send_sem=send,
            recv_sem=recv,
            device_id=device,
            device_id_type=MESH,
        )

    first_c = r * width_c
    first_r = core * (depth // 2) + (side * n_y + y) * width_r
    group_c = first_c // LANES
    group_r = first_r // LANES
    loads = [
        pltpu.make_async_copy(
            ref_factor.at[:, pl.ds(pl.multiple_of(group_r * LANES, LANES), LANES)],
            rf_block,
            load_sems.at[0],
        ),
        pltpu.make_async_copy(ref_plan, rp, load_sems.at[1]),
        pltpu.make_async_copy(
            cand_factor.at[:, pl.ds(pl.multiple_of(group_c * LANES, LANES), LANES)],
            cf_block,
            load_sems.at[2],
        ),
        pltpu.make_async_copy(cand_plan, cp, load_sems.at[3]),
        pltpu.make_async_copy(weights_in, weights, load_sems.at[4]),
        pltpu.make_async_copy(cand_factor, cf, load_sems.at[5]),
        pltpu.make_async_copy(ref_factor, rf, load_sems.at[6]),
    ]
    for load in loads:
        load.start()
    for_all(greet, greet, (1, 0))

    loads[0].wait()
    loads[1].wait()
    moment_r[...] = contract_rows(rf_block[...], rp[...]) * (1.0 / (rows_r * n_ref))
    sub_r = pl.multiple_of(first_r - group_r * LANES, width_r)
    sum_r[r] = moment_r[pl.ds(sub_r, width_r), :]
    loads[2].wait()
    loads[3].wait()
    moment_c[...] = contract_rows(cf_block[...], cp[...]) * (1.0 / (rows_c * n_cand))
    sub_c = pl.multiple_of(first_c - group_c * LANES, width_c)
    part_c[...] = moment_c[pl.ds(sub_c, width_c), :].reshape(part_c.shape)

    pl.semaphore_wait(barrier, n_cand + n_ref - 2)

    pair = remote(
        part_c.at[sibling], pair_c, pair_send.at[0], pair_recv.at[0], to_c(0, 0, 1)
    )
    pair.start()
    pair.wait_recv()
    sum_c[spot] = part_c[core] + pair_c[...]

    for_all(
        lambda device: remote(
            sum_c.at[spot], sum_c.at[spot], send_c.at[0], recv_c.at[0], device
        ).start(),
        lambda device: remote(
            sum_r.at[r], sum_r.at[r], send_r.at[0], recv_r.at[0], device
        ).start(),
        (0,),
    )

    tile = min(rows_c, rows_r, 64)

    def split_all(factor, high_ref, low_ref, rows):
        @pl.loop(0, rows, step=tile)
        def _(at):
            at = pl.multiple_of(at, tile)
            high, low = split(factor[pl.ds(at, tile), :])
            high_ref[pl.ds(at, tile), :] = high
            low_ref[pl.ds(at, tile), :] = low

    loads[5].wait()
    split_all(cf, cf_high, cf_low, rows_c)
    loads[6].wait()
    split_all(rf, rf_high, rf_low, rows_r)
    loads[4].wait()

    wait_bytes(sum_c.at[pl.ds(0, n_cand // 2 - 1)], recv_c.at[0])
    cand_moment[r, core] = jnp.sum(sum_c[...], axis=0)
    wait_bytes(sum_r.at[pl.ds(0, n_ref - 1)], recv_r.at[0])
    my_slice = ref_moment.at[pl.ds(pl.multiple_of(first_r, width_r), width_r)]
    my_slice[...] = jnp.sum(sum_r[...], axis=0)

    for_all(
        lambda device: remote(
            my_slice, my_slice, send_c.at[1], recv_c.at[1], device
        ).start(),
        lambda device: remote(
            cand_moment.at[r, core],
            cand_moment.at[r, core],
            send_r.at[1],
            recv_r.at[1],
            device,
        ).start(),
        (0,),
    )
    half = depth // 2
    my_half = ref_moment.at[pl.ds(pl.multiple_of(core * half, half), half)]
    wait_bytes(ref_moment.at[pl.ds(0, half - width_r)], recv_c.at[1])
    hand_r = remote(my_half, my_half, pair_send.at[1], pair_recv.at[1], to_c(0, 0, 1))
    hand_r.start()
    wait_bytes(cand_moment.at[pl.ds(0, n_ref - 1), core], recv_r.at[1])
    mine = cand_moment.at[:, pl.ds(core, 1)]
    hand_c = remote(mine, mine, pair_send.at[2], pair_recv.at[2], to_c(0, 0, 1))
    hand_c.start()

    weights_row = weights[...]
    weights_inverse = 1.0 / weights_row

    def gradient(high, low, moment, out, rows):
        right = jnp.concatenate(split(moment), axis=1)
        step = min(rows, 256)

        def body(i, top):
            at = pl.multiple_of(i * step, step)
            both = jnp.dot(
                high[pl.ds(at, step), :], right, preferred_element_type=F32
            ) + jnp.dot(low[pl.ds(at, step), :], right, preferred_element_type=F32)
            grad = (both[:, :LANES] + both[:, LANES:]) * weights_inverse
            out[pl.ds(at, step), :] = grad
            return jnp.maximum(top, jnp.max(jnp.abs(grad), axis=0, keepdims=True))

        return lax.fori_loop(0, rows // step, body, jnp.zeros((1, LANES), F32))

    hand_r.wait_recv()
    top_c = gradient(cf_high, cf_low, ref_moment[...], kc, rows_c)
    hand_c.wait_recv()
    all_cand_moment = cand_moment[...].reshape(depth, LANES)
    top_r = gradient(rf_high, rf_low, all_cand_moment, kr, rows_r)

    def exchange(slot, row_c, row_r):
        out_row[slot, 0] = row_c
        out_row[slot, 1] = row_r
        for_all(
            lambda device: remote(
                out_row.at[slot, 0],
                in_c.at[slot, c],
                send_c.at[2 + slot],
                recv_c.at[2 + slot],
                device,
            ).start(),
            lambda device: remote(
                out_row.at[slot, 1],
                in_r.at[slot, r],
                send_r.at[2 + slot],
                recv_r.at[2 + slot],
                device,
            ).start(),
            (1, 0),
        )
        in_c[slot, c] = row_c
        in_r[slot, r] = row_r
        wait_bytes(in_c.at[slot, pl.ds(0, n_cand - 1)], recv_c.at[2 + slot])
        wait_bytes(in_r.at[slot, pl.ds(0, n_ref - 1)], recv_r.at[2 + slot])
        return in_c[slot], in_r[slot]

    local = jnp.maximum(top_c, top_r)
    tops_c, tops_r = exchange(0, local, local)
    grad_weights = -jnp.sum(
        all_cand_moment * ref_moment[...], axis=0, keepdims=True
    ) / (weights_row * weights_row)
    tops = jnp.maximum(jnp.max(tops_c, axis=0), jnp.max(tops_r, axis=0))
    tops = jnp.maximum(tops, jnp.abs(grad_weights))
    top = jnp.max(tops, axis=1, keepdims=True) + TINY
    factor = -STEP_SIZE / top
    kernel_weights = weights_row * jnp.exp(grad_weights * factor)

    scale_c = jnp.ones((1, LANES), F32)
    scale_r = jnp.ones((1, LANES), F32)

    def row_pass(k, plan, scale, rows, first, last):
        step = min(rows, 128)

        def body(i, mass):
            at = pl.multiple_of(i * step, step)
            here = pl.ds(at, step)
            if first:
                block = plan[here, :] * jnp.exp(k[here, :] * factor)
                k[here, :] = block
                total = jnp.sum(block, axis=1, keepdims=True)
            else:
                block = k[here, :]
                total = jnp.sum(block * scale, axis=1, keepdims=True)
            scaled = block * (LANES / total)
            if last:
                k[here, :] = scaled
            return mass + jnp.sum(scaled.reshape(step // 8, 8, LANES), axis=0)

        mass = lax.fori_loop(0, rows // step, body, jnp.zeros((8, LANES), F32))
        return jnp.sum(mass, axis=0, keepdims=True)

    store_c = pltpu.make_async_copy(kc, scaled_cand, store_sems.at[0])
    store_r = pltpu.make_async_copy(kr, scaled_ref, store_sems.at[1])
    for i in range(ITERS):
        first, last = i == 0, i == ITERS - 1
        part_mass_c = row_pass(kc, cp, scale_c, rows_c, first, last)
        part_mass_r = row_pass(kr, rp, scale_r, rows_r, first, last)
        if last:
            store_c.start()
            store_r.start()
        masses_c, masses_r = exchange(1 + i, part_mass_c, part_mass_r)
        mass_c = jnp.sum(masses_c, axis=0) * (1.0 / (rows_c * n_cand))
        mass_r = jnp.sum(masses_r, axis=0) * (1.0 / (rows_r * n_ref))
        new_weights = cube_root(kernel_weights * scale_c * mass_c * scale_r * mass_r)
        scale_c = new_weights / mass_c
        scale_r = new_weights / mass_r

    rows_out[0:1] = new_weights
    rows_out[1:2] = scale_c
    rows_out[2:3] = scale_r
    store_c.wait()
    store_r.wait()

    pair.wait_send()
    hand_r.wait_send()
    hand_c.wait_send()
    wait_bytes(sum_c.at[pl.ds(0, n_cand // 2 - 1)], send_c.at[0])
    wait_bytes(sum_r.at[pl.ds(0, n_ref - 1)], send_r.at[0])
    wait_bytes(ref_moment.at[pl.ds(0, half - width_r)], send_c.at[1])
    wait_bytes(cand_moment.at[pl.ds(0, n_ref - 1), core], send_r.at[1])
    for slot in range(1 + ITERS):
        wait_bytes(in_c.at[slot, pl.ds(0, n_cand - 1)], send_c.at[2 + slot])
        wait_bytes(in_r.at[slot, pl.ds(0, n_ref - 1)], send_r.at[2 + slot])


def finish(
    scaled_cand, scaled_ref, rows, new_cand_plan, new_ref_plan, new_weights, c, r, w, sems
):
    loads = [
        pltpu.make_async_copy(rows, w, sems.at[0]),
        pltpu.make_async_copy(scaled_ref, r, sems.at[1]),
        pltpu.make_async_copy(scaled_cand, c, sems.at[2]),
    ]
    stores = [
        pltpu.make_async_copy(w.at[pl.ds(0, 1)], new_weights, sems.at[3]),
        pltpu.make_async_copy(r, new_ref_plan, sems.at[4]),
        pltpu.make_async_copy(c, new_cand_plan, sems.at[5]),
    ]
    for load in loads:
        load.start()
    loads[0].wait()
    stores[0].start()
    loads[1].wait()
    r[...] = r[...] * w[2:3]
    stores[1].start()
    loads[2].wait()
    c[...] = c[...] * w[1:2]
    stores[2].start()
    for store in stores:
        store.wait()


def on_device(n_cand, n_ref, cand_factor, ref_factor, cand_plan, ref_plan, weights):
    rows_c, depth = cand_factor.shape
    rows_r = ref_factor.shape[0]
    rank = weights.shape[0]
    width_c, width_r = depth // n_ref, depth // n_cand
    part = width_c // 2
    phases = 3 + ITERS
    hbm = pl.BlockSpec(memory_space=pltpu.HBM)
    vmem = pl.BlockSpec(memory_space=pltpu.VMEM)
    scaled_cand, scaled_ref, rows_out = pl.pallas_call(
        functools.partial(kernel, n_cand, n_ref),
        out_shape=(
            jax.ShapeDtypeStruct((rows_c, rank), F32),
            jax.ShapeDtypeStruct((rows_r, rank), F32),
            jax.ShapeDtypeStruct((8, rank), F32),
        ),
        in_specs=[hbm] * 5,
        out_specs=(hbm, hbm, vmem),
        scratch_shapes=[
            pltpu.VMEM((rows_c, depth), F32),
            pltpu.VMEM((rows_r, depth), F32),
            pltpu.VMEM((rows_c, LANES), F32),
            pltpu.VMEM((rows_r, LANES), F32),
            pltpu.VMEM((rows_c, rank), F32),
            pltpu.VMEM((rows_r, rank), F32),
            pltpu.VMEM((1, rank), F32),
            pltpu.VMEM((rows_c, depth), BF16),
            pltpu.VMEM((rows_c, depth), BF16),
            pltpu.VMEM((rows_r, depth), BF16),
            pltpu.VMEM((rows_r, depth), BF16),
            pltpu.VMEM((rows_c, rank), F32),
            pltpu.VMEM((rows_r, rank), F32),
            pltpu.VMEM((LANES, rank), F32),
            pltpu.VMEM((LANES, rank), F32),
            pltpu.VMEM((2, part, rank), F32),
            pltpu.VMEM((part, rank), F32),
            pltpu.VMEM((n_cand // 2, part, rank), F32),
            pltpu.VMEM((n_ref, width_r, rank), F32),
            pltpu.VMEM((n_ref, 2, part, rank), F32),
            pltpu.VMEM((depth, rank), F32),
            pltpu.VMEM((1 + ITERS, 2, 1, rank), F32),
            pltpu.VMEM((1 + ITERS, n_cand, 1, rank), F32),
            pltpu.VMEM((1 + ITERS, n_ref, 1, rank), F32),
            pltpu.SemaphoreType.DMA((7,)),
            pltpu.SemaphoreType.DMA((2,)),
            pltpu.SemaphoreType.DMA((3,)),
            pltpu.SemaphoreType.DMA((3,)),
            pltpu.SemaphoreType.DMA((phases,)),
            pltpu.SemaphoreType.DMA((phases,)),
            pltpu.SemaphoreType.DMA((phases,)),
            pltpu.SemaphoreType.DMA((phases,)),
        ],
        compiler_params=pltpu.CompilerParams(
            collective_id=0, has_side_effects=True, vmem_limit_bytes=60 * 2**20
        ),
    )(cand_factor, ref_factor, cand_plan, ref_plan, weights.reshape(1, rank))
    new_cand_plan, new_ref_plan, new_weights = pl.pallas_call(
        finish,
        out_shape=(
            jax.ShapeDtypeStruct((rows_c, rank), F32),
            jax.ShapeDtypeStruct((rows_r, rank), F32),
            jax.ShapeDtypeStruct((1, rank), F32),
        ),
        in_specs=[hbm] * 3,
        out_specs=(hbm, hbm, hbm),
        scratch_shapes=[
            pltpu.VMEM((rows_c, rank), F32),
            pltpu.VMEM((rows_r, rank), F32),
            pltpu.VMEM((8, rank), F32),
            pltpu.SemaphoreType.DMA((6,)),
        ],
        compiler_params=pltpu.CompilerParams(vmem_limit_bytes=60 * 2**20),
    )(scaled_cand, scaled_ref, rows_out)
    return new_cand_plan, new_ref_plan, new_weights.reshape(rank)


def solution(mesh):
    in_specs = (P("cand", None), P("ref", None), P("cand", None), P("ref", None), P())
    out_specs = (P("cand", None), P("ref", None), P())
    return jax.shard_map(
        functools.partial(on_device, mesh.shape["cand"], mesh.shape["ref"]),
        mesh=mesh,
        in_specs=in_specs,
        out_specs=out_specs,
        check_vma=False,
    )
```

```python
import functools

import jax
import jax.numpy as jnp
from jax import lax
from jax.experimental import pallas as pl
from jax.experimental.pallas import tpu as pltpu
from jax.sharding import PartitionSpec as P

ITERS = 3
STEP_SIZE = 3.0
TINY = 1e-06
LANES = 128
MESH = pl.DeviceIdType.MESH
F32 = jnp.float32
BF16 = jnp.bfloat16


def split(x):
    high = x.astype(BF16)
    return high, (x - high.astype(F32)).astype(BF16)


def contract_rows(left, right):
    both = lax.dot_general(
        jnp.concatenate(split(left), axis=1),
        jnp.concatenate(split(right), axis=1),
        (((0,), (0,)), ((), ())),
        preferred_element_type=F32,
    )
    half = left.shape[1]
    return (both[:half, :LANES] + both[half:, LANES:]) + (
        both[half:, :LANES] + both[:half, LANES:]
    )


def cube_root(x):
    y = jnp.exp(jnp.log(x) * (1.0 / 3.0))
    return y - (y * y * y - x) / (3.0 * y * y)


def wait_bytes(ref, sem):
    pltpu.make_async_copy(ref, ref, sem).wait()


def kernel(
    n_cand,
    n_ref,
    cand_factor,
    ref_factor,
    cand_plan,
    ref_plan,
    weights_in,
    scaled_cand,
    scaled_ref,
    rows_out,
    cf,
    rf,
    cp,
    rp,
    weights,
    cf_high,
    cf_low,
    rf_high,
    rf_low,
    kc,
    kr,
    moment_c,
    moment_r,
    part_c,
    pair_c,
    sum_c,
    sum_r,
    cand_moment,
    ref_moment,
    out_row,
    in_c,
    in_r,
    load_sems,
    rest_sems,
    pair_send,
    pair_recv,
    send_c,
    send_r,
    recv_c,
    recv_r,
):
    c = lax.axis_index("cand")
    r = lax.axis_index("ref")
    n_y, n_z = n_cand // 4, n_ref // 2
    core = lax.rem(c, 2)
    y = lax.rem(c // 2, n_y)
    x_lo = c // (2 * n_y)
    x_hi = lax.rem(r, 2)
    z = r // 2
    spot = x_lo * n_y + y
    side = lax.rem(x_lo + x_hi, 2)
    groups, rows_c, _ = cf.shape
    rows_r = rf.shape[1]
    depth = groups * LANES
    half = depth // 2
    width_c = depth // n_ref
    width_r = depth // n_cand
    part = width_c // 2
    sibling = 1 - core

    def away(step, size):
        turn = lax.rem(step, 2) * 2 - 1
        return lax.rem(size // 2 + turn * ((step + 1) // 2) + size, size)

    def to_c(flip, offset_y, flip_core):
        new_x = lax.rem(x_lo + flip, 2)
        new_core = lax.rem(core + flip_core, 2)
        return ((new_x * n_y + lax.rem(y + offset_y, n_y)) * 2 + new_core, r)

    def to_r(flip, offset_z):
        new_c = (lax.rem(x_lo + flip, 2) * n_y + y) * 2 + core
        return (new_c, lax.rem(z + offset_z, n_z) * 2 + lax.rem(x_hi + flip, 2))

    def for_all(visit_c, visit_r, cores):
        def body(step, _):
            offset_y = away(step, n_y)
            for flip in (1, 0):
                for flip_core in cores:
                    visit_c(to_c(flip, offset_y, flip_core))
            if n_z == n_y:
                for flip in (1, 0):
                    visit_r(to_r(flip, offset_y))
            return 0

        lax.fori_loop(0, n_y - 1, body, 0)
        if n_z != n_y:

            def body_r(step, _):
                for flip in (1, 0):
                    visit_r(to_r(flip, away(step, n_z)))
                return 0

            lax.fori_loop(0, n_z - 1, body_r, 0)
        for flip_core in cores:
            visit_c(to_c(1, 0, flip_core))
        visit_r(to_r(1, 0))
        if 1 in cores:
            visit_c(to_c(0, 0, 1))

    barrier = pltpu.get_barrier_semaphore()

    def greet(device):
        pl.semaphore_signal(barrier, inc=1, device_id=device, device_id_type=MESH)

    def remote(source, target, send, recv, device):
        return pltpu.make_async_remote_copy(
            src_ref=source,
            dst_ref=target,
            send_sem=send,
            recv_sem=recv,
            device_id=device,
            device_id_type=MESH,
        )

    first_c = r * width_c
    first_r = core * (depth // 2) + (side * n_y + y) * width_r
    group_c = first_c // LANES
    group_r = first_r // LANES
    for_all(greet, greet, (1, 0))

    def columns(factor, group, target, sem):
        at = pl.ds(pl.multiple_of(group * LANES, LANES), LANES)
        return pltpu.make_async_copy(factor.at[:, at], target.at[group], sem)

    loads = [
        columns(ref_factor, group_r, rf, load_sems.at[0]),
        pltpu.make_async_copy(ref_plan, rp, load_sems.at[1]),
        columns(cand_factor, group_c, cf, load_sems.at[2]),
        pltpu.make_async_copy(cand_plan, cp, load_sems.at[3]),
        pltpu.make_async_copy(weights_in, weights, load_sems.at[4]),
    ]
    for load in loads:
        load.start()
    rest = [
        columns(cand_factor, lax.rem(group_c + i, groups), cf, rest_sems.at[0, i])
        for i in range(1, groups)
    ] + [
        columns(ref_factor, lax.rem(group_r + i, groups), rf, rest_sems.at[1, i])
        for i in range(1, groups)
    ]

    loads[0].wait()
    loads[1].wait()
    moment_r[...] = contract_rows(rf[group_r], rp[...]) * (1.0 / (rows_r * n_ref))
    sub_r = pl.multiple_of(first_r - group_r * LANES, width_r)
    sum_r[r] = moment_r[pl.ds(sub_r, width_r), :]
    loads[2].wait()
    loads[3].wait()
    for load in rest:
        load.start()
    moment_c[...] = contract_rows(cf[group_c], cp[...]) * (1.0 / (rows_c * n_cand))
    sub_c = pl.multiple_of(first_c - group_c * LANES, width_c)
    part_c[...] = moment_c[pl.ds(sub_c, width_c), :].reshape(part_c.shape)

    pl.semaphore_wait(barrier, n_cand + n_ref - 2)

    pair = remote(
        part_c.at[sibling], pair_c, pair_send.at[0], pair_recv.at[0], to_c(0, 0, 1)
    )
    pair.start()
    pair.wait_recv()
    sum_c[spot] = part_c[core] + pair_c[...]

    for_all(
        lambda device: remote(
            sum_c.at[spot], sum_c.at[spot], send_c.at[0], recv_c.at[0], device
        ).start(),
        lambda device: remote(
            sum_r.at[r], sum_r.at[r], send_r.at[0], recv_r.at[0], device
        ).start(),
        (0,),
    )

    def split_all(factor, high_ref, low_ref, rows):
        tile = min(rows, 128)
        for group in range(groups):
            side_of, at = divmod(group * LANES, half)

            @pl.loop(0, rows // tile)
            def _(i):
                here = pl.ds(pl.multiple_of(i * tile, tile), tile)
                high, low = split(factor[group, here, :])
                high_ref[side_of, here, at : at + LANES] = high
                low_ref[side_of, here, at : at + LANES] = low

    for load in rest:
        load.wait()
    split_all(cf, cf_high, cf_low, rows_c)
    split_all(rf, rf_high, rf_low, rows_r)
    loads[4].wait()

    wait_bytes(sum_c.at[pl.ds(0, n_cand // 2 - 1)], recv_c.at[0])
    cand_moment[r, core] = jnp.sum(sum_c[...], axis=0)
    wait_bytes(sum_r.at[pl.ds(0, n_ref - 1)], recv_r.at[0])
    my_slice = ref_moment.at[pl.ds(pl.multiple_of(first_r, width_r), width_r)]
    my_slice[...] = jnp.sum(sum_r[...], axis=0)

    for_all(
        lambda device: remote(
            my_slice, my_slice, send_c.at[1], recv_c.at[1], device
        ).start(),
        lambda device: remote(
            cand_moment.at[r, core],
            cand_moment.at[r, core],
            send_r.at[1],
            recv_r.at[1],
            device,
        ).start(),
        (0,),
    )
    my_half = ref_moment.at[pl.ds(pl.multiple_of(core * half, half), half)]
    wait_bytes(ref_moment.at[pl.ds(0, half - width_r)], recv_c.at[1])
    hand_r = remote(my_half, my_half, pair_send.at[1], pair_recv.at[1], to_c(0, 0, 1))
    hand_r.start()
    wait_bytes(cand_moment.at[pl.ds(0, n_ref - 1), core], recv_r.at[1])
    mine = cand_moment.at[:, pl.ds(core, 1)]
    hand_c = remote(mine, mine, pair_send.at[2], pair_recv.at[2], to_c(0, 0, 1))
    hand_c.start()

    weights_row = weights[...]
    weights_inverse = 1.0 / weights_row

    def right_side(moment):
        return jnp.concatenate(split(moment), axis=1)

    def product(high, low, which, here, right):
        both = jnp.dot(
            high[which, here, :], right, preferred_element_type=F32
        ) + jnp.dot(low[which, here, :], right, preferred_element_type=F32)
        return both[:, :LANES] + both[:, LANES:]

    def tiles(rows, step):
        return [pl.ds(at, step) for at in range(0, rows, step)]

    def peak(top, grad):
        return jnp.maximum(
            top, jnp.max(jnp.abs(grad).reshape(-1, 8, LANES), axis=0)
        )

    step_c, step_r = min(rows_c, 256), min(rows_r, 256)
    right = right_side(my_half[...])
    for here in tiles(rows_c, step_c):
        kc[here, :] = product(cf_high, cf_low, core, here, right)
    tops = jnp.zeros((8, LANES), F32)
    hand_r.wait_recv()
    other = ref_moment[pl.ds(pl.multiple_of(sibling * half, half), half), :]
    right = right_side(other)
    for here in tiles(rows_c, step_c):
        grad = kc[here, :] + product(cf_high, cf_low, sibling, here, right)
        grad = grad * weights_inverse
        kc[here, :] = grad
        tops = peak(tops, grad)
    hand_c.wait_recv()
    all_cand_moment = cand_moment[...].reshape(depth, LANES)
    rights = [right_side(all_cand_moment[:half]), right_side(all_cand_moment[half:])]
    for here in tiles(rows_r, step_r):
        grad = product(rf_high, rf_low, 0, here, rights[0]) + product(
            rf_high, rf_low, 1, here, rights[1]
        )
        grad = grad * weights_inverse
        kr[here, :] = grad
        tops = peak(tops, grad)
    local = jnp.max(tops, axis=0, keepdims=True)

    def exchange(slot, row_c, row_r):
        out_row[slot, 0] = row_c
        out_row[slot, 1] = row_r
        for_all(
            lambda device: remote(
                out_row.at[slot, 0],
                in_c.at[slot, c],
                send_c.at[2 + slot],
                recv_c.at[2 + slot],
                device,
            ).start(),
            lambda device: remote(
                out_row.at[slot, 1],
                in_r.at[slot, r],
                send_r.at[2 + slot],
                recv_r.at[2 + slot],
                device,
            ).start(),
            (1, 0),
        )
        in_c[slot, c] = row_c
        in_r[slot, r] = row_r
        wait_bytes(in_c.at[slot, pl.ds(0, n_cand - 1)], recv_c.at[2 + slot])
        wait_bytes(in_r.at[slot, pl.ds(0, n_ref - 1)], recv_r.at[2 + slot])
        return in_c[slot], in_r[slot]

    tops_c, tops_r = exchange(0, local, local)
    grad_weights = -jnp.sum(
        all_cand_moment * ref_moment[...], axis=0, keepdims=True
    ) / (weights_row * weights_row)
    tops = jnp.maximum(jnp.max(tops_c, axis=0), jnp.max(tops_r, axis=0))
    tops = jnp.maximum(tops, jnp.abs(grad_weights))
    top = jnp.max(tops, axis=1, keepdims=True) + TINY
    factor = -STEP_SIZE / top
    kernel_weights = weights_row * jnp.exp(grad_weights * factor)

    scale_c = jnp.ones((1, LANES), F32)
    scale_r = jnp.ones((1, LANES), F32)

    def row_pass(k, plan, scale, first, to):
        rows = k.shape[0]
        mass = jnp.zeros((8, LANES), F32)
        for here in tiles(rows, min(rows, 128)):
            if first:
                block = plan[here, :] * jnp.exp(k[here, :] * factor)
                k[here, :] = block
                total = jnp.sum(block, axis=1, keepdims=True)
            else:
                block = k[here, :]
                total = jnp.sum(block * scale, axis=1, keepdims=True)
            scaled = block * (LANES / total)
            if to is not None:
                to[here, :] = scaled
            mass = mass + jnp.sum(scaled.reshape(-1, 8, LANES), axis=0)
        return jnp.sum(mass, axis=0, keepdims=True)

    for i in range(ITERS):
        first, last = i == 0, i == ITERS - 1
        part_mass_c = row_pass(kc, cp, scale_c, first, scaled_cand if last else None)
        part_mass_r = row_pass(kr, rp, scale_r, first, scaled_ref if last else None)
        masses_c, masses_r = exchange(1 + i, part_mass_c, part_mass_r)
        mass_c = jnp.sum(masses_c, axis=0) * (1.0 / (rows_c * n_cand))
        mass_r = jnp.sum(masses_r, axis=0) * (1.0 / (rows_r * n_ref))
        new_weights = cube_root(kernel_weights * scale_c * mass_c * scale_r * mass_r)
        scale_c = new_weights / mass_c
        scale_r = new_weights / mass_r

    rows_out[0:1] = new_weights
    rows_out[1:2] = scale_c
    rows_out[2:3] = scale_r

    pair.wait_send()
    hand_r.wait_send()
    hand_c.wait_send()
    wait_bytes(sum_c.at[pl.ds(0, n_cand // 2 - 1)], send_c.at[0])
    wait_bytes(sum_r.at[pl.ds(0, n_ref - 1)], send_r.at[0])
    wait_bytes(ref_moment.at[pl.ds(0, half - width_r)], send_c.at[1])
    wait_bytes(cand_moment.at[pl.ds(0, n_ref - 1), core], send_r.at[1])
    for slot in range(1 + ITERS):
        wait_bytes(in_c.at[slot, pl.ds(0, n_cand - 1)], send_c.at[2 + slot])
        wait_bytes(in_r.at[slot, pl.ds(0, n_ref - 1)], send_r.at[2 + slot])


def finish(
    scaled_cand, scaled_ref, rows, new_cand_plan, new_ref_plan, new_weights, c, r, sems
):
    rows_c, rows_r = c.shape[0], r.shape[0]
    pieces = [
        (scaled_cand, c, new_cand_plan, 1, pl.ds(i * rows_c // 2, rows_c // 2))
        for i in range(2)
    ] + [(scaled_ref, r, new_ref_plan, 2, pl.ds(0, rows_r))]
    stores = [
        pltpu.make_async_copy(rows.at[pl.ds(0, 1)], new_weights, sems.at[len(pieces)])
    ]
    stores[0].start()
    for i, (source, scratch, target, row, here) in enumerate(pieces):
        scratch[here, :] = source[here, :] * rows[row : row + 1]
        store = pltpu.make_async_copy(scratch.at[here], target.at[here], sems.at[i])
        store.start()
        stores.append(store)
    for store in stores:
        store.wait()


def on_device(n_cand, n_ref, cand_factor, ref_factor, cand_plan, ref_plan, weights):
    rows_c, depth = cand_factor.shape
    rows_r = ref_factor.shape[0]
    rank = weights.shape[0]
    width_c, width_r = depth // n_ref, depth // n_cand
    part = width_c // 2
    phases = 3 + ITERS
    hbm = pl.BlockSpec(memory_space=pltpu.HBM)
    held = [
        pltpu.with_memory_space_constraint(x, pltpu.HBM)
        for x in (cand_factor, ref_factor, cand_plan, ref_plan, weights.reshape(1, rank))
    ]
    vmem = pl.BlockSpec(memory_space=pltpu.VMEM)
    scaled_cand, scaled_ref, rows_out = pl.pallas_call(
        functools.partial(kernel, n_cand, n_ref),
        out_shape=(
            pltpu.VMEM((rows_c, rank), F32),
            pltpu.VMEM((rows_r, rank), F32),
            pltpu.VMEM((8, rank), F32),
        ),
        in_specs=[hbm] * 5,
        out_specs=(vmem, vmem, vmem),
        scratch_shapes=[
            pltpu.VMEM((depth // LANES, rows_c, LANES), F32),
            pltpu.VMEM((depth // LANES, rows_r, LANES), F32),
            pltpu.VMEM((rows_c, rank), F32),
            pltpu.VMEM((rows_r, rank), F32),
            pltpu.VMEM((1, rank), F32),
            pltpu.VMEM((2, rows_c, depth // 2), BF16),
            pltpu.VMEM((2, rows_c, depth // 2), BF16),
            pltpu.VMEM((2, rows_r, depth // 2), BF16),
            pltpu.VMEM((2, rows_r, depth // 2), BF16),
            pltpu.VMEM((rows_c, rank), F32),
            pltpu.VMEM((rows_r, rank), F32),
            pltpu.VMEM((LANES, rank), F32),
            pltpu.VMEM((LANES, rank), F32),
            pltpu.VMEM((2, part, rank), F32),
            pltpu.VMEM((part, rank), F32),
            pltpu.VMEM((n_cand // 2, part, rank), F32),
            pltpu.VMEM((n_ref, width_r, rank), F32),
            pltpu.VMEM((n_ref, 2, part, rank), F32),
            pltpu.VMEM((depth, rank), F32),
            pltpu.VMEM((1 + ITERS, 2, 1, rank), F32),
            pltpu.VMEM((1 + ITERS, n_cand, 1, rank), F32),
            pltpu.VMEM((1 + ITERS, n_ref, 1, rank), F32),
            pltpu.SemaphoreType.DMA((5,)),
            pltpu.SemaphoreType.DMA((2, depth // LANES)),
            pltpu.SemaphoreType.DMA((3,)),
            pltpu.SemaphoreType.DMA((3,)),
            pltpu.SemaphoreType.DMA((phases,)),
            pltpu.SemaphoreType.DMA((phases,)),
            pltpu.SemaphoreType.DMA((phases,)),
            pltpu.SemaphoreType.DMA((phases,)),
        ],
        compiler_params=pltpu.CompilerParams(
            collective_id=0, has_side_effects=True, vmem_limit_bytes=32 * 2**20
        ),
    )(*held)
    new_cand_plan, new_ref_plan, new_weights = pl.pallas_call(
        finish,
        out_shape=(
            jax.ShapeDtypeStruct((rows_c, rank), F32),
            jax.ShapeDtypeStruct((rows_r, rank), F32),
            jax.ShapeDtypeStruct((1, rank), F32),
        ),
        in_specs=[vmem] * 3,
        out_specs=(hbm, hbm, hbm),
        scratch_shapes=[
            pltpu.VMEM((rows_c, rank), F32),
            pltpu.VMEM((rows_r, rank), F32),
            pltpu.SemaphoreType.DMA((4,)),
        ],
        compiler_params=pltpu.CompilerParams(vmem_limit_bytes=16 * 2**20),
    )(
        *(
            pltpu.with_memory_space_constraint(x, pltpu.VMEM)
            for x in (scaled_cand, scaled_ref, rows_out)
        )
    )
    return new_cand_plan, new_ref_plan, new_weights.reshape(rank)


def solution(mesh):
    in_specs = (P("cand", None), P("ref", None), P("cand", None), P("ref", None), P())
    out_specs = (P("cand", None), P("ref", None), P())
    return jax.shard_map(
        functools.partial(on_device, mesh.shape["cand"], mesh.shape["ref"]),
        mesh=mesh,
        in_specs=in_specs,
        out_specs=out_specs,
        check_vma=False,
    )
```

```python
import functools

import jax
import jax.numpy as jnp
from jax import lax
from jax.experimental import pallas as pl
from jax.experimental.pallas import tpu as pltpu
from jax.sharding import PartitionSpec as P

ITERS = 3
STEP_SIZE = 3.0
TINY = 1e-06
LANES = 128
MESH = pl.DeviceIdType.MESH
F32 = jnp.float32
BF16 = jnp.bfloat16


def split(x):
    high = x.astype(BF16)
    return high, (x - high.astype(F32)).astype(BF16)


def contract_rows(left, right):
    both = lax.dot_general(
        jnp.concatenate(split(left), axis=1),
        jnp.concatenate(split(right), axis=1),
        (((0,), (0,)), ((), ())),
        preferred_element_type=F32,
    )
    half = left.shape[1]
    return (both[:half, :LANES] + both[half:, LANES:]) + (
        both[half:, :LANES] + both[:half, LANES:]
    )


def cube_root(x):
    slope = 1.0 / (3.0 * x)
    y = jnp.exp(jnp.log(x) * (1.0 / 3.0))
    return y - y * ((y * y * y - x) * slope)


def add_up(rows):
    terms = [rows[i] for i in range(rows.shape[0])]
    while len(terms) > 1:
        pairs = [a + b for a, b in zip(terms[::2], terms[1::2])]
        terms = pairs + terms[len(pairs) * 2 :]
    return terms[0]


def wait_bytes(ref, sem):
    pltpu.make_async_copy(ref, ref, sem).wait()


def kernel(
    n_cand,
    n_ref,
    cand_factor,
    ref_factor,
    cand_plan,
    ref_plan,
    weights_in,
    scaled_cand,
    scaled_ref,
    rows_out,
    cf,
    rf,
    cp,
    rp,
    weights,
    cf_high,
    cf_low,
    rf_high,
    rf_low,
    kc,
    kr,
    moment_c,
    moment_r,
    part_c,
    pair_c,
    sum_c,
    sum_r,
    cand_moment,
    ref_moment,
    out_row,
    in_c,
    in_r,
    load_sems,
    rest_sems,
    pair_send,
    pair_recv,
    send_c,
    send_r,
    recv_c,
    recv_r,
):
    c = lax.axis_index("cand")
    r = lax.axis_index("ref")
    n_y, n_z = n_cand // 4, n_ref // 2
    core = lax.rem(c, 2)
    y = lax.rem(c // 2, n_y)
    x_lo = c // (2 * n_y)
    x_hi = lax.rem(r, 2)
    z = r // 2
    spot = x_lo * n_y + y
    side = lax.rem(x_lo + x_hi, 2)
    groups, rows_c, _ = cf.shape
    rows_r = rf.shape[1]
    depth = groups * LANES
    half = depth // 2
    width_c = depth // n_ref
    width_r = depth // n_cand
    part = width_c // 2
    sibling = 1 - core

    def away(step, size):
        turn = lax.rem(step, 2) * 2 - 1
        return lax.rem(size // 2 + turn * ((step + 1) // 2) + size, size)

    def to_c(flip, offset_y, flip_core):
        new_x = lax.rem(x_lo + flip, 2)
        new_core = lax.rem(core + flip_core, 2)
        return ((new_x * n_y + lax.rem(y + offset_y, n_y)) * 2 + new_core, r)

    def to_r(flip, offset_z):
        new_c = (lax.rem(x_lo + flip, 2) * n_y + y) * 2 + core
        return (new_c, lax.rem(z + offset_z, n_z) * 2 + lax.rem(x_hi + flip, 2))

    def for_all(visit_c, visit_r, cores):
        def body(step, _):
            offset_y = away(step, n_y)
            for flip in (1, 0):
                if visit_c:
                    for flip_core in cores:
                        visit_c(to_c(flip, offset_y, flip_core))
                if visit_r and n_z == n_y:
                    visit_r(to_r(flip, offset_y))
            return 0

        lax.fori_loop(0, n_y - 1, body, 0)
        if visit_r and n_z != n_y:

            def body_r(step, _):
                for flip in (1, 0):
                    visit_r(to_r(flip, away(step, n_z)))
                return 0

            lax.fori_loop(0, n_z - 1, body_r, 0)
        if visit_c:
            for flip_core in cores:
                visit_c(to_c(1, 0, flip_core))
        if visit_r:
            visit_r(to_r(1, 0))
        if visit_c and 1 in cores:
            visit_c(to_c(0, 0, 1))

    barrier = pltpu.get_barrier_semaphore()

    def greet(device):
        pl.semaphore_signal(barrier, inc=1, device_id=device, device_id_type=MESH)

    def remote(source, target, send, recv, device):
        return pltpu.make_async_remote_copy(
            src_ref=source,
            dst_ref=target,
            send_sem=send,
            recv_sem=recv,
            device_id=device,
            device_id_type=MESH,
        )

    first_c = r * width_c
    first_r = core * (depth // 2) + (side * n_y + y) * width_r
    group_c = first_c // LANES
    group_r = first_r // LANES
    def columns(factor, group, target, sem):
        at = pl.ds(pl.multiple_of(group * LANES, LANES), LANES)
        return pltpu.make_async_copy(factor.at[:, at], target.at[group], sem)

    loads = [
        columns(ref_factor, group_r, rf, load_sems.at[0]),
        pltpu.make_async_copy(ref_plan, rp, load_sems.at[1]),
        columns(cand_factor, group_c, cf, load_sems.at[2]),
        pltpu.make_async_copy(cand_plan, cp, load_sems.at[3]),
        pltpu.make_async_copy(weights_in, weights, load_sems.at[4]),
    ]
    for load in loads:
        load.start()
    for_all(greet, greet, (1, 0))
    rest = [
        columns(cand_factor, lax.rem(group_c + i, groups), cf, rest_sems.at[0, i])
        for i in range(1, groups)
    ] + [
        columns(ref_factor, lax.rem(group_r + i, groups), rf, rest_sems.at[1, i])
        for i in range(1, groups)
    ]

    loads[0].wait()
    loads[1].wait()
    moment_r[...] = contract_rows(rf[group_r], rp[...]) * (1.0 / (rows_r * n_ref))
    sub_r = pl.multiple_of(first_r - group_r * LANES, width_r)
    sum_r[r] = moment_r[pl.ds(sub_r, width_r), :]
    loads[2].wait()
    loads[3].wait()
    for load in rest:
        load.start()
    moment_c[...] = contract_rows(cf[group_c], cp[...]) * (1.0 / (rows_c * n_cand))
    sub_c = pl.multiple_of(first_c - group_c * LANES, width_c)
    part_c[...] = moment_c[pl.ds(sub_c, width_c), :].reshape(part_c.shape)

    pl.semaphore_wait(barrier, n_cand + n_ref - 2)

    pair = remote(
        part_c.at[sibling], pair_c, pair_send.at[0], pair_recv.at[0], to_c(0, 0, 1)
    )
    pair.start()

    for_all(
        None,
        lambda device: remote(
            sum_r.at[r], sum_r.at[r], send_r.at[0], recv_r.at[0], device
        ).start(),
        (0,),
    )
    pair.wait_recv()
    sum_c[spot] = part_c[core] + pair_c[...]
    for_all(
        lambda device: remote(
            sum_c.at[spot], sum_c.at[spot], send_c.at[0], recv_c.at[0], device
        ).start(),
        None,
        (0,),
    )

    def split_all(factor, high_ref, low_ref, rows):
        tile = min(rows, 128)
        for group in range(groups):
            side_of, at = divmod(group * LANES, half)

            @pl.loop(0, rows // tile)
            def _(i):
                here = pl.ds(pl.multiple_of(i * tile, tile), tile)
                high, low = split(factor[group, here, :])
                high_ref[side_of, here, at : at + LANES] = high
                low_ref[side_of, here, at : at + LANES] = low

    for load in rest:
        load.wait()
    split_all(cf, cf_high, cf_low, rows_c)
    split_all(rf, rf_high, rf_low, rows_r)
    loads[4].wait()

    wait_bytes(sum_r.at[pl.ds(0, n_ref - 1)], recv_r.at[0])
    my_slice = ref_moment.at[pl.ds(pl.multiple_of(first_r, width_r), width_r)]
    my_slice[...] = jnp.sum(sum_r[...], axis=0)
    for_all(
        lambda device: remote(
            my_slice, my_slice, send_c.at[1], recv_c.at[1], device
        ).start(),
        None,
        (0,),
    )
    wait_bytes(sum_c.at[pl.ds(0, n_cand // 2 - 1)], recv_c.at[0])
    cand_moment[r, core] = jnp.sum(sum_c[...], axis=0)
    for_all(
        None,
        lambda device: remote(
            cand_moment.at[r, core],
            cand_moment.at[r, core],
            send_r.at[1],
            recv_r.at[1],
            device,
        ).start(),
        (0,),
    )
    my_half = ref_moment.at[pl.ds(pl.multiple_of(core * half, half), half)]
    wait_bytes(ref_moment.at[pl.ds(0, half - width_r)], recv_c.at[1])
    hand_r = remote(my_half, my_half, pair_send.at[1], pair_recv.at[1], to_c(0, 0, 1))
    hand_r.start()
    mine = cand_moment.at[:, pl.ds(core, 1)]
    hand_c = remote(mine, mine, pair_send.at[2], pair_recv.at[2], to_c(0, 0, 1))

    weights_row = weights[...]
    weights_inverse = 1.0 / weights_row

    def right_side(moment):
        return jnp.concatenate(split(moment), axis=1)

    def product(high, low, which, here, right):
        both = jnp.dot(
            high[which, here, :], right, preferred_element_type=F32
        ) + jnp.dot(low[which, here, :], right, preferred_element_type=F32)
        return both[:, :LANES] + both[:, LANES:]

    def tiles(rows, step):
        return [pl.ds(at, step) for at in range(0, rows, step)]

    def peak(top, grad):
        return jnp.maximum(
            top, jnp.max(jnp.abs(grad).reshape(-1, 8, LANES), axis=0)
        )

    step_c, step_r = min(rows_c, 256), min(rows_r, 256)
    right = right_side(my_half[...])
    for here in tiles(rows_c, step_c):
        kc[here, :] = product(cf_high, cf_low, core, here, right)
    tops = jnp.zeros((8, LANES), F32)
    hand_r.wait_recv()
    wait_bytes(cand_moment.at[pl.ds(0, n_ref - 1), core], recv_r.at[1])
    hand_c.start()
    other = ref_moment[pl.ds(pl.multiple_of(sibling * half, half), half), :]
    right = right_side(other)
    for here in tiles(rows_c, step_c):
        grad = kc[here, :] + product(cf_high, cf_low, sibling, here, right)
        grad = grad * weights_inverse
        kc[here, :] = grad
        tops = peak(tops, grad)
    hand_c.wait_recv()
    all_cand_moment = cand_moment[...].reshape(depth, LANES)
    rights = [right_side(all_cand_moment[:half]), right_side(all_cand_moment[half:])]
    for here in tiles(rows_r, step_r):
        grad = product(rf_high, rf_low, 0, here, rights[0]) + product(
            rf_high, rf_low, 1, here, rights[1]
        )
        grad = grad * weights_inverse
        kr[here, :] = grad
        tops = peak(tops, grad)
    local = jnp.max(tops, axis=0, keepdims=True)

    def sent(slot):
        if slot == 0:
            pair.wait_send()
            wait_bytes(sum_c.at[pl.ds(0, n_cand // 2 - 1)], send_c.at[0])
            wait_bytes(sum_r.at[pl.ds(0, n_ref - 1)], send_r.at[0])
        elif slot == 1:
            hand_r.wait_send()
            hand_c.wait_send()
            wait_bytes(ref_moment.at[pl.ds(0, half - width_r)], send_c.at[1])
            wait_bytes(cand_moment.at[pl.ds(0, n_ref - 1), core], send_r.at[1])

    def rows_sent(slot):
        wait_bytes(in_c.at[slot, pl.ds(0, n_cand - 1)], send_c.at[2 + slot])
        wait_bytes(in_r.at[slot, pl.ds(0, n_ref - 1)], send_r.at[2 + slot])

    def exchange(slot, row_c, row_r):
        out_row[slot, 0] = row_c
        out_row[slot, 1] = row_r
        for_all(
            lambda device: remote(
                out_row.at[slot, 0],
                in_c.at[slot, c],
                send_c.at[2 + slot],
                recv_c.at[2 + slot],
                device,
            ).start(),
            lambda device: remote(
                out_row.at[slot, 1],
                in_r.at[slot, r],
                send_r.at[2 + slot],
                recv_r.at[2 + slot],
                device,
            ).start(),
            (1, 0),
        )
        in_c[slot, c] = row_c
        in_r[slot, r] = row_r
        sent(slot)
        if slot > 0:
            rows_sent(slot - 1)
        wait_bytes(in_c.at[slot, pl.ds(0, n_cand - 1)], recv_c.at[2 + slot])
        wait_bytes(in_r.at[slot, pl.ds(0, n_ref - 1)], recv_r.at[2 + slot])
        return in_c[slot], in_r[slot]

    tops_c, tops_r = exchange(0, local, local)
    grad_weights = -jnp.sum(
        all_cand_moment * ref_moment[...], axis=0, keepdims=True
    ) / (weights_row * weights_row)
    tops = jnp.maximum(jnp.max(tops_c, axis=0), jnp.max(tops_r, axis=0))
    tops = jnp.maximum(tops, jnp.abs(grad_weights))
    top = jnp.max(tops, axis=1, keepdims=True) + TINY
    factor = -STEP_SIZE / top
    kernel_weights = weights_row * jnp.exp(grad_weights * factor)

    scale_c = jnp.ones((1, LANES), F32)
    scale_r = jnp.ones((1, LANES), F32)

    def row_pass(k, plan, scale, first, to):
        rows = k.shape[0]
        mass = jnp.zeros((8, LANES), F32)
        for here in tiles(rows, min(rows, 128)):
            if first:
                block = plan[here, :] * jnp.exp(k[here, :] * factor)
                k[here, :] = block
                total = jnp.sum(block, axis=1, keepdims=True)
            else:
                block = k[here, :]
                total = jnp.sum(block * scale, axis=1, keepdims=True)
            scaled = block * (LANES / total)
            if to is not None:
                to[here, :] = scaled
            mass = mass + jnp.sum(scaled.reshape(-1, 8, LANES), axis=0)
        return jnp.sum(mass, axis=0, keepdims=True)

    for i in range(ITERS):
        first, last = i == 0, i == ITERS - 1
        part_mass_c = row_pass(kc, cp, scale_c, first, scaled_cand if last else None)
        part_mass_r = row_pass(kr, rp, scale_r, first, scaled_ref if last else None)
        masses_c, masses_r = exchange(1 + i, part_mass_c, part_mass_r)
        mass_c = add_up(masses_c) * (1.0 / (rows_c * n_cand))
        mass_r = add_up(masses_r) * (1.0 / (rows_r * n_ref))
        new_weights = cube_root(kernel_weights * scale_c * mass_c * scale_r * mass_r)
        scale_c = new_weights / mass_c
        scale_r = new_weights / mass_r

    rows_out[0:1] = new_weights
    rows_out[1:2] = scale_c
    rows_out[2:3] = scale_r

    rows_sent(ITERS)


def finish(
    scaled_cand, scaled_ref, rows, new_cand_plan, new_ref_plan, new_weights, c, r, sems
):
    rows_c, rows_r = c.shape[0], r.shape[0]
    pieces = [
        (scaled_cand, c, new_cand_plan, 1, pl.ds(i * rows_c // 4, rows_c // 4))
        for i in range(4)
    ] + [
        (scaled_ref, r, new_ref_plan, 2, pl.ds(i * rows_r // 2, rows_r // 2))
        for i in range(2)
    ]
    stores = [
        pltpu.make_async_copy(rows.at[pl.ds(0, 1)], new_weights, sems.at[len(pieces)])
    ]
    stores[0].start()
    for i, (source, scratch, target, row, here) in enumerate(pieces):
        scratch[here, :] = source[here, :] * rows[row : row + 1]
        store = pltpu.make_async_copy(scratch.at[here], target.at[here], sems.at[i])
        store.start()
        stores.append(store)
    for store in stores:
        store.wait()


def on_device(n_cand, n_ref, cand_factor, ref_factor, cand_plan, ref_plan, weights):
    rows_c, depth = cand_factor.shape
    rows_r = ref_factor.shape[0]
    rank = weights.shape[0]
    width_c, width_r = depth // n_ref, depth // n_cand
    part = width_c // 2
    phases = 3 + ITERS
    hbm = pl.BlockSpec(memory_space=pltpu.HBM)
    held = [
        pltpu.with_memory_space_constraint(x, pltpu.HBM)
        for x in (cand_factor, ref_factor, cand_plan, ref_plan, weights.reshape(1, rank))
    ]
    vmem = pl.BlockSpec(memory_space=pltpu.VMEM)
    scaled_cand, scaled_ref, rows_out = pl.pallas_call(
        functools.partial(kernel, n_cand, n_ref),
        out_shape=(
            pltpu.VMEM((rows_c, rank), F32),
            pltpu.VMEM((rows_r, rank), F32),
            pltpu.VMEM((8, rank), F32),
        ),
        in_specs=[hbm] * 5,
        out_specs=(vmem, vmem, vmem),
        scratch_shapes=[
            pltpu.VMEM((depth // LANES, rows_c, LANES), F32),
            pltpu.VMEM((depth // LANES, rows_r, LANES), F32),
            pltpu.VMEM((rows_c, rank), F32),
            pltpu.VMEM((rows_r, rank), F32),
            pltpu.VMEM((1, rank), F32),
            pltpu.VMEM((2, rows_c, depth // 2), BF16),
            pltpu.VMEM((2, rows_c, depth // 2), BF16),
            pltpu.VMEM((2, rows_r, depth // 2), BF16),
            pltpu.VMEM((2, rows_r, depth // 2), BF16),
            pltpu.VMEM((rows_c, rank), F32),
            pltpu.VMEM((rows_r, rank), F32),
            pltpu.VMEM((LANES, rank), F32),
            pltpu.VMEM((LANES, rank), F32),
            pltpu.VMEM((2, part, rank), F32),
            pltpu.VMEM((part, rank), F32),
            pltpu.VMEM((n_cand // 2, part, rank), F32),
            pltpu.VMEM((n_ref, width_r, rank), F32),
            pltpu.VMEM((n_ref, 2, part, rank), F32),
            pltpu.VMEM((depth, rank), F32),
            pltpu.VMEM((1 + ITERS, 2, 1, rank), F32),
            pltpu.VMEM((1 + ITERS, n_cand, 1, rank), F32),
            pltpu.VMEM((1 + ITERS, n_ref, 1, rank), F32),
            pltpu.SemaphoreType.DMA((5,)),
            pltpu.SemaphoreType.DMA((2, depth // LANES)),
            pltpu.SemaphoreType.DMA((3,)),
            pltpu.SemaphoreType.DMA((3,)),
            pltpu.SemaphoreType.DMA((phases,)),
            pltpu.SemaphoreType.DMA((phases,)),
            pltpu.SemaphoreType.DMA((phases,)),
            pltpu.SemaphoreType.DMA((phases,)),
        ],
        compiler_params=pltpu.CompilerParams(
            collective_id=0, has_side_effects=True, vmem_limit_bytes=32 * 2**20
        ),
    )(*held)
    new_cand_plan, new_ref_plan, new_weights = pl.pallas_call(
        finish,
        out_shape=(
            jax.ShapeDtypeStruct((rows_c, rank), F32),
            jax.ShapeDtypeStruct((rows_r, rank), F32),
            jax.ShapeDtypeStruct((1, rank), F32),
        ),
        in_specs=[vmem] * 3,
        out_specs=(hbm, hbm, hbm),
        scratch_shapes=[
            pltpu.VMEM((rows_c, rank), F32),
            pltpu.VMEM((rows_r, rank), F32),
            pltpu.SemaphoreType.DMA((7,)),
        ],
        compiler_params=pltpu.CompilerParams(vmem_limit_bytes=16 * 2**20),
    )(
        *(
            pltpu.with_memory_space_constraint(x, pltpu.VMEM)
            for x in (scaled_cand, scaled_ref, rows_out)
        )
    )
    return new_cand_plan, new_ref_plan, new_weights.reshape(rank)


def solution(mesh):
    in_specs = (P("cand", None), P("ref", None), P("cand", None), P("ref", None), P())
    out_specs = (P("cand", None), P("ref", None), P())
    return jax.shard_map(
        functools.partial(on_device, mesh.shape["cand"], mesh.shape["ref"]),
        mesh=mesh,
        in_specs=in_specs,
        out_specs=out_specs,
        check_vma=False,
    )
```

```python
import functools

import jax
import jax.numpy as jnp
from jax import lax
from jax.experimental import pallas as pl
from jax.experimental.pallas import tpu as pltpu
from jax.sharding import PartitionSpec as P

ITERS = 3
STEP_SIZE = 3.0
TINY = 1e-06
LANES = 128
MESH = pl.DeviceIdType.MESH
F32 = jnp.float32
BF16 = jnp.bfloat16


def split(x):
    high = x.astype(BF16)
    return high, (x - high.astype(F32)).astype(BF16)


def contract_rows(left, right):
    both = lax.dot_general(
        jnp.concatenate(split(left), axis=1),
        jnp.concatenate(split(right), axis=1),
        (((0,), (0,)), ((), ())),
        preferred_element_type=F32,
    )
    half = left.shape[1]
    return (both[:half, :LANES] + both[half:, LANES:]) + (
        both[half:, :LANES] + both[:half, LANES:]
    )


def cube_root(x):
    slope = 1.0 / (3.0 * x)
    y = jnp.exp(jnp.log(x) * (1.0 / 3.0))
    return y - y * ((y * y * y - x) * slope)


def add_up(rows):
    terms = [rows[i] for i in range(rows.shape[0])]
    while len(terms) > 1:
        pairs = [a + b for a, b in zip(terms[::2], terms[1::2])]
        terms = pairs + terms[len(pairs) * 2 :]
    return terms[0]


def wait_bytes(ref, sem):
    pltpu.make_async_copy(ref, ref, sem).wait()


def kernel(
    n_cand,
    n_ref,
    cand_factor,
    ref_factor,
    cand_plan,
    ref_plan,
    weights_in,
    scaled_cand,
    scaled_ref,
    rows_out,
    cf,
    rf,
    cp,
    rp,
    weights,
    cf_high,
    cf_low,
    rf_high,
    rf_low,
    kc,
    kr,
    moment_c,
    moment_r,
    part_c,
    pair_c,
    sum_c,
    sum_r,
    cand_moment,
    ref_moment,
    out_row,
    in_c,
    in_r,
    load_sems,
    rest_sems,
    pair_send,
    pair_recv,
    send_c,
    send_r,
    recv_c,
    recv_r,
):
    c = lax.axis_index("cand")
    r = lax.axis_index("ref")
    n_y, n_z = n_cand // 4, n_ref // 2
    core = lax.rem(c, 2)
    y = lax.rem(c // 2, n_y)
    x_lo = c // (2 * n_y)
    x_hi = lax.rem(r, 2)
    z = r // 2
    spot = x_lo * n_y + y
    side = lax.rem(x_lo + x_hi, 2)
    groups, rows_c, _ = cf.shape
    rows_r = rf.shape[1]
    depth = groups * LANES
    half = depth // 2
    width_c = depth // n_ref
    width_r = depth // n_cand
    part = width_c // 2
    sibling = 1 - core

    def to_c(flip, offset_y, flip_core):
        new_x = lax.rem(x_lo + flip, 2)
        new_core = lax.rem(core + flip_core, 2)
        return ((new_x * n_y + lax.rem(y + offset_y, n_y)) * 2 + new_core, r)

    def to_r(flip, offset_z):
        new_c = (lax.rem(x_lo + flip, 2) * n_y + y) * 2 + core
        return (new_c, lax.rem(z + offset_z, n_z) * 2 + lax.rem(x_hi + flip, 2))

    def for_all(visit_c, visit_r, cores):
        def ring(size):
            order = sorted(range(1, size), key=lambda d: -min(d, size - d))
            return [(d, flip) for d in order for flip in (1, 0)]

        for offset, flip in ring(n_y):
            if visit_c:
                for flip_core in cores:
                    visit_c(to_c(flip, offset, flip_core))
            if visit_r and n_z == n_y:
                visit_r(to_r(flip, offset))
        if visit_r and n_z != n_y:
            for offset, flip in ring(n_z):
                visit_r(to_r(flip, offset))
        if visit_c:
            for flip_core in cores:
                visit_c(to_c(1, 0, flip_core))
        if visit_r:
            visit_r(to_r(1, 0))
        if visit_c and 1 in cores:
            visit_c(to_c(0, 0, 1))

    barrier = pltpu.get_barrier_semaphore()

    def greet(device):
        pl.semaphore_signal(barrier, inc=1, device_id=device, device_id_type=MESH)

    def remote(source, target, send, recv, device):
        return pltpu.make_async_remote_copy(
            src_ref=source,
            dst_ref=target,
            send_sem=send,
            recv_sem=recv,
            device_id=device,
            device_id_type=MESH,
        )

    first_c = r * width_c
    first_r = core * (depth // 2) + (side * n_y + y) * width_r
    group_c = first_c // LANES
    group_r = first_r // LANES
    def columns(factor, group, target, sem):
        at = pl.ds(pl.multiple_of(group * LANES, LANES), LANES)
        return pltpu.make_async_copy(factor.at[:, at], target.at[group], sem)

    loads = [
        columns(ref_factor, group_r, rf, load_sems.at[0]),
        pltpu.make_async_copy(ref_plan, rp, load_sems.at[1]),
        columns(cand_factor, group_c, cf, load_sems.at[2]),
        pltpu.make_async_copy(cand_plan, cp, load_sems.at[3]),
        pltpu.make_async_copy(weights_in, weights, load_sems.at[4]),
    ]
    for load in loads:
        load.start()
    for_all(greet, greet, (1, 0))
    rest = [
        columns(cand_factor, lax.rem(group_c + i, groups), cf, rest_sems.at[0, i])
        for i in range(1, groups)
    ] + [
        columns(ref_factor, lax.rem(group_r + i, groups), rf, rest_sems.at[1, i])
        for i in range(1, groups)
    ]

    loads[0].wait()
    loads[1].wait()
    moment_r[...] = contract_rows(rf[group_r], rp[...]) * (1.0 / (rows_r * n_ref))
    sub_r = pl.multiple_of(first_r - group_r * LANES, width_r)
    sum_r[r] = moment_r[pl.ds(sub_r, width_r), :]
    loads[2].wait()
    loads[3].wait()
    for load in rest:
        load.start()
    moment_c[...] = contract_rows(cf[group_c], cp[...]) * (1.0 / (rows_c * n_cand))
    sub_c = pl.multiple_of(first_c - group_c * LANES, width_c)
    part_c[...] = moment_c[pl.ds(sub_c, width_c), :].reshape(part_c.shape)

    pl.semaphore_wait(barrier, n_cand + n_ref - 2)

    pair = remote(
        part_c.at[sibling], pair_c, pair_send.at[0], pair_recv.at[0], to_c(0, 0, 1)
    )
    pair.start()

    for_all(
        None,
        lambda device: remote(
            sum_r.at[r], sum_r.at[r], send_r.at[0], recv_r.at[0], device
        ).start(),
        (0,),
    )
    pair.wait_recv()
    sum_c[spot] = part_c[core] + pair_c[...]
    for_all(
        lambda device: remote(
            sum_c.at[spot], sum_c.at[spot], send_c.at[0], recv_c.at[0], device
        ).start(),
        None,
        (0,),
    )

    def split_all(factor, high_ref, low_ref, rows):
        tile = min(rows, 128)
        for group in range(groups):
            side_of, at = divmod(group * LANES, half)

            @pl.loop(0, rows // tile)
            def _(i):
                here = pl.ds(pl.multiple_of(i * tile, tile), tile)
                high, low = split(factor[group, here, :])
                high_ref[side_of, here, at : at + LANES] = high
                low_ref[side_of, here, at : at + LANES] = low

    for load in rest:
        load.wait()
    split_all(cf, cf_high, cf_low, rows_c)
    split_all(rf, rf_high, rf_low, rows_r)
    loads[4].wait()

    wait_bytes(sum_r.at[pl.ds(0, n_ref - 1)], recv_r.at[0])
    my_slice = ref_moment.at[pl.ds(pl.multiple_of(first_r, width_r), width_r)]
    my_slice[...] = jnp.sum(sum_r[...], axis=0)
    for_all(
        lambda device: remote(
            my_slice, my_slice, send_c.at[1], recv_c.at[1], device
        ).start(),
        None,
        (0,),
    )
    wait_bytes(sum_c.at[pl.ds(0, n_cand // 2 - 1)], recv_c.at[0])
    cand_moment[r, core] = jnp.sum(sum_c[...], axis=0)
    for_all(
        None,
        lambda device: remote(
            cand_moment.at[r, core],
            cand_moment.at[r, core],
            send_r.at[1],
            recv_r.at[1],
            device,
        ).start(),
        (0,),
    )
    my_half = ref_moment.at[pl.ds(pl.multiple_of(core * half, half), half)]
    wait_bytes(ref_moment.at[pl.ds(0, half - width_r)], recv_c.at[1])
    hand_r = remote(my_half, my_half, pair_send.at[1], pair_recv.at[1], to_c(0, 0, 1))
    hand_r.start()
    mine = cand_moment.at[:, pl.ds(core, 1)]
    hand_c = remote(mine, mine, pair_send.at[2], pair_recv.at[2], to_c(0, 0, 1))

    weights_row = weights[...]
    weights_inverse = 1.0 / weights_row

    def right_side(moment):
        return jnp.concatenate(split(moment), axis=1)

    def product(high, low, which, here, right):
        both = jnp.dot(
            high[which, here, :], right, preferred_element_type=F32
        ) + jnp.dot(low[which, here, :], right, preferred_element_type=F32)
        return both[:, :LANES] + both[:, LANES:]

    def tiles(rows, step):
        return [pl.ds(at, step) for at in range(0, rows, step)]

    def peak(top, grad):
        return jnp.maximum(
            top, jnp.max(jnp.abs(grad).reshape(-1, 8, LANES), axis=0)
        )

    step_c, step_r = min(rows_c, 256), min(rows_r, 256)
    right = right_side(my_half[...])
    for here in tiles(rows_c, step_c):
        kc[here, :] = product(cf_high, cf_low, core, here, right)
    tops = jnp.zeros((8, LANES), F32)
    hand_r.wait_recv()
    wait_bytes(cand_moment.at[pl.ds(0, n_ref - 1), core], recv_r.at[1])
    hand_c.start()
    other = ref_moment[pl.ds(pl.multiple_of(sibling * half, half), half), :]
    right = right_side(other)
    for here in tiles(rows_c, step_c):
        grad = kc[here, :] + product(cf_high, cf_low, sibling, here, right)
        grad = grad * weights_inverse
        kc[here, :] = grad
        tops = peak(tops, grad)
    hand_c.wait_recv()
    all_cand_moment = cand_moment[...].reshape(depth, LANES)
    rights = [right_side(all_cand_moment[:half]), right_side(all_cand_moment[half:])]
    for here in tiles(rows_r, step_r):
        grad = product(rf_high, rf_low, 0, here, rights[0]) + product(
            rf_high, rf_low, 1, here, rights[1]
        )
        grad = grad * weights_inverse
        kr[here, :] = grad
        tops = peak(tops, grad)
    local = jnp.max(tops, axis=0, keepdims=True)

    def sent(slot):
        if slot == 0:
            pair.wait_send()
            wait_bytes(sum_c.at[pl.ds(0, n_cand // 2 - 1)], send_c.at[0])
            wait_bytes(sum_r.at[pl.ds(0, n_ref - 1)], send_r.at[0])
        elif slot == 1:
            hand_r.wait_send()
            hand_c.wait_send()
            wait_bytes(ref_moment.at[pl.ds(0, half - width_r)], send_c.at[1])
            wait_bytes(cand_moment.at[pl.ds(0, n_ref - 1), core], send_r.at[1])

    def rows_sent(slot):
        wait_bytes(in_c.at[slot, pl.ds(0, n_cand - 1)], send_c.at[2 + slot])
        wait_bytes(in_r.at[slot, pl.ds(0, n_ref - 1)], send_r.at[2 + slot])

    def exchange(slot, row_c, row_r):
        out_row[slot, 0] = row_c
        out_row[slot, 1] = row_r
        for_all(
            lambda device: remote(
                out_row.at[slot, 0],
                in_c.at[slot, c],
                send_c.at[2 + slot],
                recv_c.at[2 + slot],
                device,
            ).start(),
            lambda device: remote(
                out_row.at[slot, 1],
                in_r.at[slot, r],
                send_r.at[2 + slot],
                recv_r.at[2 + slot],
                device,
            ).start(),
            (1, 0),
        )
        in_c[slot, c] = row_c
        in_r[slot, r] = row_r
        sent(slot)
        if slot > 0:
            rows_sent(slot - 1)
        wait_bytes(in_c.at[slot, pl.ds(0, n_cand - 1)], recv_c.at[2 + slot])
        wait_bytes(in_r.at[slot, pl.ds(0, n_ref - 1)], recv_r.at[2 + slot])
        return in_c[slot], in_r[slot]

    tops_c, tops_r = exchange(0, local, local)
    grad_weights = -jnp.sum(
        all_cand_moment * ref_moment[...], axis=0, keepdims=True
    ) / (weights_row * weights_row)
    tops = jnp.maximum(jnp.max(tops_c, axis=0), jnp.max(tops_r, axis=0))
    tops = jnp.maximum(tops, jnp.abs(grad_weights))
    top = jnp.max(tops, axis=1, keepdims=True) + TINY
    factor = -STEP_SIZE / top
    kernel_weights = weights_row * jnp.exp(grad_weights * factor)

    scale_c = jnp.ones((1, LANES), F32)
    scale_r = jnp.ones((1, LANES), F32)

    def row_pass(k, plan, scale, first, to):
        rows = k.shape[0]
        mass = jnp.zeros((8, LANES), F32)
        for here in tiles(rows, min(rows, 128)):
            if first:
                block = plan[here, :] * jnp.exp(k[here, :] * factor)
                k[here, :] = block
                total = jnp.sum(block, axis=1, keepdims=True)
            else:
                block = k[here, :]
                total = jnp.sum(block * scale, axis=1, keepdims=True)
            scaled = block * (LANES / total)
            if to is not None:
                to[here, :] = scaled
            mass = mass + jnp.sum(scaled.reshape(-1, 8, LANES), axis=0)
        return jnp.sum(mass, axis=0, keepdims=True)

    for i in range(ITERS):
        first, last = i == 0, i == ITERS - 1
        part_mass_c = row_pass(kc, cp, scale_c, first, scaled_cand if last else None)
        part_mass_r = row_pass(kr, rp, scale_r, first, scaled_ref if last else None)
        masses_c, masses_r = exchange(1 + i, part_mass_c, part_mass_r)
        mass_c = add_up(masses_c) * (1.0 / (rows_c * n_cand))
        mass_r = add_up(masses_r) * (1.0 / (rows_r * n_ref))
        new_weights = cube_root(kernel_weights * scale_c * mass_c * scale_r * mass_r)
        scale_c = new_weights / mass_c
        scale_r = new_weights / mass_r

    rows_out[0:1] = new_weights
    rows_out[1:2] = scale_c
    rows_out[2:3] = scale_r

    rows_sent(ITERS)


def finish(
    scaled_cand, scaled_ref, rows, new_cand_plan, new_ref_plan, new_weights, c, r, sems
):
    rows_c, rows_r = c.shape[0], r.shape[0]
    pieces = [
        (scaled_cand, c, new_cand_plan, 1, pl.ds(i * rows_c // 4, rows_c // 4))
        for i in range(4)
    ] + [
        (scaled_ref, r, new_ref_plan, 2, pl.ds(i * rows_r // 2, rows_r // 2))
        for i in range(2)
    ]
    stores = [
        pltpu.make_async_copy(rows.at[pl.ds(0, 1)], new_weights, sems.at[len(pieces)])
    ]
    stores[0].start()
    for i, (source, scratch, target, row, here) in enumerate(pieces):
        scratch[here, :] = source[here, :] * rows[row : row + 1]
        store = pltpu.make_async_copy(scratch.at[here], target.at[here], sems.at[i])
        store.start()
        stores.append(store)
    for store in stores:
        store.wait()


def on_device(n_cand, n_ref, cand_factor, ref_factor, cand_plan, ref_plan, weights):
    rows_c, depth = cand_factor.shape
    rows_r = ref_factor.shape[0]
    rank = weights.shape[0]
    width_c, width_r = depth // n_ref, depth // n_cand
    part = width_c // 2
    phases = 3 + ITERS
    hbm = pl.BlockSpec(memory_space=pltpu.HBM)
    held = [
        pltpu.with_memory_space_constraint(x, pltpu.HBM)
        for x in (cand_factor, ref_factor, cand_plan, ref_plan, weights.reshape(1, rank))
    ]
    vmem = pl.BlockSpec(memory_space=pltpu.VMEM)
    scaled_cand, scaled_ref, rows_out = pl.pallas_call(
        functools.partial(kernel, n_cand, n_ref),
        out_shape=(
            pltpu.VMEM((rows_c, rank), F32),
            pltpu.VMEM((rows_r, rank), F32),
            pltpu.VMEM((8, rank), F32),
        ),
        in_specs=[hbm] * 5,
        out_specs=(vmem, vmem, vmem),
        scratch_shapes=[
            pltpu.VMEM((depth // LANES, rows_c, LANES), F32),
            pltpu.VMEM((depth // LANES, rows_r, LANES), F32),
            pltpu.VMEM((rows_c, rank), F32),
            pltpu.VMEM((rows_r, rank), F32),
            pltpu.VMEM((1, rank), F32),
            pltpu.VMEM((2, rows_c, depth // 2), BF16),
            pltpu.VMEM((2, rows_c, depth // 2), BF16),
            pltpu.VMEM((2, rows_r, depth // 2), BF16),
            pltpu.VMEM((2, rows_r, depth // 2), BF16),
            pltpu.VMEM((rows_c, rank), F32),
            pltpu.VMEM((rows_r, rank), F32),
            pltpu.VMEM((LANES, rank), F32),
            pltpu.VMEM((LANES, rank), F32),
            pltpu.VMEM((2, part, rank), F32),
            pltpu.VMEM((part, rank), F32),
            pltpu.VMEM((n_cand // 2, part, rank), F32),
            pltpu.VMEM((n_ref, width_r, rank), F32),
            pltpu.VMEM((n_ref, 2, part, rank), F32),
            pltpu.VMEM((depth, rank), F32),
            pltpu.VMEM((1 + ITERS, 2, 1, rank), F32),
            pltpu.VMEM((1 + ITERS, n_cand, 1, rank), F32),
            pltpu.VMEM((1 + ITERS, n_ref, 1, rank), F32),
            pltpu.SemaphoreType.DMA((5,)),
            pltpu.SemaphoreType.DMA((2, depth // LANES)),
            pltpu.SemaphoreType.DMA((3,)),
            pltpu.SemaphoreType.DMA((3,)),
            pltpu.SemaphoreType.DMA((phases,)),
            pltpu.SemaphoreType.DMA((phases,)),
            pltpu.SemaphoreType.DMA((phases,)),
            pltpu.SemaphoreType.DMA((phases,)),
        ],
        compiler_params=pltpu.CompilerParams(
            collective_id=0, has_side_effects=True, vmem_limit_bytes=32 * 2**20
        ),
    )(*held)
    new_cand_plan, new_ref_plan, new_weights = pl.pallas_call(
        finish,
        out_shape=(
            jax.ShapeDtypeStruct((rows_c, rank), F32),
            jax.ShapeDtypeStruct((rows_r, rank), F32),
            jax.ShapeDtypeStruct((1, rank), F32),
        ),
        in_specs=[vmem] * 3,
        out_specs=(hbm, hbm, hbm),
        scratch_shapes=[
            pltpu.VMEM((rows_c, rank), F32),
            pltpu.VMEM((rows_r, rank), F32),
            pltpu.SemaphoreType.DMA((7,)),
        ],
        compiler_params=pltpu.CompilerParams(vmem_limit_bytes=16 * 2**20),
    )(
        *(
            pltpu.with_memory_space_constraint(x, pltpu.VMEM)
            for x in (scaled_cand, scaled_ref, rows_out)
        )
    )
    return new_cand_plan, new_ref_plan, new_weights.reshape(rank)


def solution(mesh):
    in_specs = (P("cand", None), P("ref", None), P("cand", None), P("ref", None), P())
    out_specs = (P("cand", None), P("ref", None), P())
    return jax.shard_map(
        functools.partial(on_device, mesh.shape["cand"], mesh.shape["ref"]),
        mesh=mesh,
        in_specs=in_specs,
        out_specs=out_specs,
        check_vma=False,
    )
```

```python
import functools

import jax
import jax.numpy as jnp
from jax import lax
from jax.experimental import pallas as pl
from jax.experimental.pallas import tpu as pltpu
from jax.sharding import PartitionSpec as P

ITERS = 3
STEP_SIZE = 3.0
TINY = 1e-06
LANES = 128
MESH = pl.DeviceIdType.MESH
F32 = jnp.float32
BF16 = jnp.bfloat16


def split(x):
    high = x.astype(BF16)
    return high, (x - high.astype(F32)).astype(BF16)


def contract_rows(left, right):
    both = lax.dot_general(
        jnp.concatenate(split(left), axis=1),
        jnp.concatenate(split(right), axis=1),
        (((0,), (0,)), ((), ())),
        preferred_element_type=F32,
    )
    half = left.shape[1]
    return (both[:half, :LANES] + both[half:, LANES:]) + (
        both[half:, :LANES] + both[:half, LANES:]
    )


def cube_root(x):
    slope = 1.0 / (3.0 * x)
    y = jnp.exp(jnp.log(x) * (1.0 / 3.0))
    return y - y * ((y * y * y - x) * slope)


def add_up(rows):
    terms = [rows[i] for i in range(rows.shape[0])]
    while len(terms) > 1:
        pairs = [a + b for a, b in zip(terms[::2], terms[1::2])]
        terms = pairs + terms[len(pairs) * 2 :]
    return terms[0]


def wait_bytes(ref, sem):
    pltpu.make_async_copy(ref, ref, sem).wait()


def kernel(
    n_cand,
    n_ref,
    cand_factor,
    ref_factor,
    cand_plan,
    ref_plan,
    weights_in,
    scaled_cand,
    scaled_ref,
    rows_out,
    cf,
    rf,
    cp,
    rp,
    weights,
    cf_high,
    cf_low,
    rf_high,
    rf_low,
    kc,
    kr,
    moment_c,
    moment_r,
    part_c,
    pair_c,
    sum_c,
    sum_r,
    cand_moment,
    ref_moment,
    out_row,
    in_c,
    in_r,
    load_sems,
    rest_sems,
    pair_send,
    pair_recv,
    send_c,
    send_r,
    recv_c,
    recv_r,
):
    c = lax.axis_index("cand")
    r = lax.axis_index("ref")
    n_y, n_z = n_cand // 4, n_ref // 2
    core = lax.rem(c, 2)
    y = lax.rem(c // 2, n_y)
    x_lo = c // (2 * n_y)
    x_hi = lax.rem(r, 2)
    z = r // 2
    spot = x_lo * n_y + y
    side = lax.rem(x_lo + x_hi, 2)
    groups, rows_c, _ = cf.shape
    rows_r = rf.shape[1]
    depth = groups * LANES
    half = depth // 2
    width_c = depth // n_ref
    width_r = depth // n_cand
    part = width_c // 2
    sibling = 1 - core

    def to_c(flip, offset_y, flip_core):
        new_x = lax.rem(x_lo + flip, 2)
        new_core = lax.rem(core + flip_core, 2)
        return ((new_x * n_y + lax.rem(y + offset_y, n_y)) * 2 + new_core, r)

    def to_r(flip, offset_z):
        new_c = (lax.rem(x_lo + flip, 2) * n_y + y) * 2 + core
        return (new_c, lax.rem(z + offset_z, n_z) * 2 + lax.rem(x_hi + flip, 2))

    def for_all(visit_c, visit_r, cores):
        def ring(size):
            order = sorted(range(1, size), key=lambda d: -min(d, size - d))
            return [(d, flip) for d in order for flip in (1, 0)]

        for offset, flip in ring(n_y):
            if visit_c:
                for flip_core in cores:
                    visit_c(to_c(flip, offset, flip_core))
            if visit_r and n_z == n_y:
                visit_r(to_r(flip, offset))
        if visit_r and n_z != n_y:
            for offset, flip in ring(n_z):
                visit_r(to_r(flip, offset))
        if visit_c:
            for flip_core in cores:
                visit_c(to_c(1, 0, flip_core))
        if visit_r:
            visit_r(to_r(1, 0))
        if visit_c and 1 in cores:
            visit_c(to_c(0, 0, 1))

    barrier = pltpu.get_barrier_semaphore()

    def greet(device):
        pl.semaphore_signal(barrier, inc=1, device_id=device, device_id_type=MESH)

    def remote(source, target, send, recv, device):
        return pltpu.make_async_remote_copy(
            src_ref=source,
            dst_ref=target,
            send_sem=send,
            recv_sem=recv,
            device_id=device,
            device_id_type=MESH,
        )

    first_c = r * width_c
    first_r = core * (depth // 2) + (side * n_y + y) * width_r
    group_c = first_c // LANES
    group_r = first_r // LANES
    def columns(factor, group, target, sem):
        at = pl.ds(pl.multiple_of(group * LANES, LANES), LANES)
        return pltpu.make_async_copy(factor.at[:, at], target.at[group], sem)

    loads = [
        columns(ref_factor, group_r, rf, load_sems.at[0]),
        pltpu.make_async_copy(ref_plan, rp, load_sems.at[1]),
        columns(cand_factor, group_c, cf, load_sems.at[2]),
        pltpu.make_async_copy(cand_plan, cp, load_sems.at[3]),
        pltpu.make_async_copy(weights_in, weights, load_sems.at[4]),
    ]
    for load in loads:
        load.start()
    for_all(greet, greet, (1, 0))
    rest = [
        columns(cand_factor, lax.rem(group_c + i, groups), cf, rest_sems.at[0, i])
        for i in range(1, groups)
    ] + [
        columns(ref_factor, lax.rem(group_r + i, groups), rf, rest_sems.at[1, i])
        for i in range(1, groups)
    ]

    loads[0].wait()
    loads[1].wait()
    moment_r[...] = contract_rows(rf[group_r], rp[...]) * (1.0 / (rows_r * n_ref))
    sub_r = pl.multiple_of(first_r - group_r * LANES, width_r)
    sum_r[r] = moment_r[pl.ds(sub_r, width_r), :]
    loads[2].wait()
    loads[3].wait()
    for load in rest:
        load.start()
    moment_c[...] = contract_rows(cf[group_c], cp[...]) * (1.0 / (rows_c * n_cand))
    sub_c = pl.multiple_of(first_c - group_c * LANES, width_c)
    part_c[...] = moment_c[pl.ds(sub_c, width_c), :].reshape(part_c.shape)

    pl.semaphore_wait(barrier, n_cand + n_ref - 2)

    pair = remote(
        part_c.at[sibling], pair_c, pair_send.at[0], pair_recv.at[0], to_c(0, 0, 1)
    )
    pair.start()

    for_all(
        None,
        lambda device: remote(
            sum_r.at[r], sum_r.at[r], send_r.at[0], recv_r.at[0], device
        ).start(),
        (0,),
    )
    pair.wait_recv()
    sum_c[spot] = part_c[core] + pair_c[...]
    for_all(
        lambda device: remote(
            sum_c.at[spot], sum_c.at[spot], send_c.at[0], recv_c.at[0], device
        ).start(),
        None,
        (0,),
    )

    def split_all(factor, high_ref, low_ref, rows):
        tile = min(rows, 128)
        for group in range(groups):
            side_of, at = divmod(group * LANES, half)

            @pl.loop(0, rows // tile)
            def _(i):
                here = pl.ds(pl.multiple_of(i * tile, tile), tile)
                high, low = split(factor[group, here, :])
                high_ref[side_of, here, at : at + LANES] = high
                low_ref[side_of, here, at : at + LANES] = low

    for load in rest:
        load.wait()
    split_all(cf, cf_high, cf_low, rows_c)
    split_all(rf, rf_high, rf_low, rows_r)
    loads[4].wait()

    wait_bytes(sum_r.at[pl.ds(0, n_ref - 1)], recv_r.at[0])
    my_slice = ref_moment.at[pl.ds(pl.multiple_of(first_r, width_r), width_r)]
    my_slice[...] = jnp.sum(sum_r[...], axis=0)
    for_all(
        lambda device: remote(
            my_slice, my_slice, send_c.at[1], recv_c.at[1], device
        ).start(),
        None,
        (0,),
    )
    wait_bytes(sum_c.at[pl.ds(0, n_cand // 2 - 1)], recv_c.at[0])
    cand_moment[r, core] = jnp.sum(sum_c[...], axis=0)
    for_all(
        None,
        lambda device: remote(
            cand_moment.at[r, core],
            cand_moment.at[r, core],
            send_r.at[1],
            recv_r.at[1],
            device,
        ).start(),
        (0,),
    )
    my_half = ref_moment.at[pl.ds(pl.multiple_of(core * half, half), half)]
    wait_bytes(ref_moment.at[pl.ds(0, half - width_r)], recv_c.at[1])
    hand_r = remote(my_half, my_half, pair_send.at[1], pair_recv.at[1], to_c(0, 0, 1))
    hand_r.start()
    mine = cand_moment.at[:, pl.ds(core, 1)]
    hand_c = remote(mine, mine, pair_send.at[2], pair_recv.at[2], to_c(0, 0, 1))

    weights_row = weights[...]
    weights_inverse = 1.0 / weights_row

    def right_side(moment):
        return jnp.concatenate(split(moment), axis=1)

    def product(high, low, which, here, right):
        both = jnp.dot(
            high[which, here, :], right, preferred_element_type=F32
        ) + jnp.dot(low[which, here, :], right, preferred_element_type=F32)
        return both[:, :LANES] + both[:, LANES:]

    def tiles(rows, step):
        return [pl.ds(at, step) for at in range(0, rows, step)]

    def peak(top, grad):
        return jnp.maximum(
            top, jnp.max(jnp.abs(grad).reshape(-1, 8, LANES), axis=0)
        )

    step_c, step_r = min(rows_c, 256), min(rows_r, 256)
    right = right_side(my_half[...])
    for here in tiles(rows_c, step_c):
        kc[here, :] = product(cf_high, cf_low, core, here, right)
    tops = jnp.zeros((8, LANES), F32)
    hand_r.wait_recv()
    wait_bytes(cand_moment.at[pl.ds(0, n_ref - 1), core], recv_r.at[1])
    hand_c.start()
    other = ref_moment[pl.ds(pl.multiple_of(sibling * half, half), half), :]
    right = right_side(other)
    for here in tiles(rows_c, step_c):
        grad = kc[here, :] + product(cf_high, cf_low, sibling, here, right)
        grad = grad * weights_inverse
        kc[here, :] = grad
        tops = peak(tops, grad)
    hand_c.wait_recv()
    all_cand_moment = cand_moment[...].reshape(depth, LANES)
    rights = [right_side(all_cand_moment[:half]), right_side(all_cand_moment[half:])]
    for here in tiles(rows_r, step_r):
        grad = product(rf_high, rf_low, 0, here, rights[0]) + product(
            rf_high, rf_low, 1, here, rights[1]
        )
        grad = grad * weights_inverse
        kr[here, :] = grad
        tops = peak(tops, grad)
    local = jnp.max(tops, axis=0, keepdims=True)

    def sent(slot):
        if slot == 0:
            pair.wait_send()
            wait_bytes(sum_c.at[pl.ds(0, n_cand // 2 - 1)], send_c.at[0])
            wait_bytes(sum_r.at[pl.ds(0, n_ref - 1)], send_r.at[0])
        elif slot == 1:
            hand_r.wait_send()
            hand_c.wait_send()
            wait_bytes(ref_moment.at[pl.ds(0, half - width_r)], send_c.at[1])
            wait_bytes(cand_moment.at[pl.ds(0, n_ref - 1), core], send_r.at[1])

    def rows_sent(slot):
        wait_bytes(in_c.at[slot, pl.ds(0, n_cand - 1)], send_c.at[2 + slot])
        wait_bytes(in_r.at[slot, pl.ds(0, n_ref - 1)], send_r.at[2 + slot])

    def exchange(slot, row_c, row_r):
        out_row[slot, 0] = row_c
        out_row[slot, 1] = row_r
        for_all(
            lambda device: remote(
                out_row.at[slot, 0],
                in_c.at[slot, c],
                send_c.at[2 + slot],
                recv_c.at[2 + slot],
                device,
            ).start(),
            lambda device: remote(
                out_row.at[slot, 1],
                in_r.at[slot, r],
                send_r.at[2 + slot],
                recv_r.at[2 + slot],
                device,
            ).start(),
            (1, 0),
        )
        in_c[slot, c] = row_c
        in_r[slot, r] = row_r
        sent(slot)
        if slot > 0:
            rows_sent(slot - 1)
        wait_bytes(in_c.at[slot, pl.ds(0, n_cand - 1)], recv_c.at[2 + slot])
        wait_bytes(in_r.at[slot, pl.ds(0, n_ref - 1)], recv_r.at[2 + slot])
        return in_c[slot], in_r[slot]

    tops_c, tops_r = exchange(0, local, local)
    grad_weights = -jnp.sum(
        all_cand_moment * ref_moment[...], axis=0, keepdims=True
    ) / (weights_row * weights_row)
    tops = jnp.maximum(jnp.max(tops_c, axis=0), jnp.max(tops_r, axis=0))
    tops = jnp.maximum(tops, jnp.abs(grad_weights))
    top = jnp.max(tops, axis=1, keepdims=True) + TINY
    factor = -STEP_SIZE / top
    kernel_weights = weights_row * jnp.exp(grad_weights * factor)

    scale_c = jnp.ones((1, LANES), F32)
    scale_r = jnp.ones((1, LANES), F32)

    def row_sums(block, by_matmul):
        if not by_matmul:
            return jnp.sum(block, axis=1, keepdims=True)
        high, low = split(block)
        ones = jnp.ones((LANES, LANES), BF16)
        return jnp.dot(high, ones, preferred_element_type=F32) + jnp.dot(
            low, ones, preferred_element_type=F32
        )

    def row_pass(k, plan, scale, first, to, by_matmul):
        rows = k.shape[0]
        mass = jnp.zeros((8, LANES), F32)
        for here in tiles(rows, min(rows, 128)):
            if first:
                block = plan[here, :] * jnp.exp(k[here, :] * factor)
                k[here, :] = block
                total = row_sums(block, by_matmul)
            else:
                block = k[here, :]
                total = row_sums(block * scale, by_matmul)
            scaled = block * (LANES / total)
            if to is not None:
                to[here, :] = scaled
            mass = mass + jnp.sum(scaled.reshape(-1, 8, LANES), axis=0)
        return jnp.sum(mass, axis=0, keepdims=True)

    for i in range(ITERS):
        first, last = i == 0, i == ITERS - 1
        part_mass_c = row_pass(
            kc, cp, scale_c, first, scaled_cand if last else None, False
        )
        part_mass_r = row_pass(
            kr, rp, scale_r, first, scaled_ref if last else None, True
        )
        masses_c, masses_r = exchange(1 + i, part_mass_c, part_mass_r)
        mass_c = add_up(masses_c) * (1.0 / (rows_c * n_cand))
        mass_r = add_up(masses_r) * (1.0 / (rows_r * n_ref))
        new_weights = cube_root(kernel_weights * scale_c * mass_c * scale_r * mass_r)
        scale_c = new_weights / mass_c
        scale_r = new_weights / mass_r

    rows_out[0:1] = new_weights
    rows_out[1:2] = scale_c
    rows_out[2:3] = scale_r

    rows_sent(ITERS)


def finish(
    scaled_cand, scaled_ref, rows, new_cand_plan, new_ref_plan, new_weights, c, r, sems
):
    rows_c, rows_r = c.shape[0], r.shape[0]
    pieces = [
        (scaled_cand, c, new_cand_plan, 1, pl.ds(i * rows_c // 4, rows_c // 4))
        for i in range(4)
    ] + [
        (scaled_ref, r, new_ref_plan, 2, pl.ds(i * rows_r // 2, rows_r // 2))
        for i in range(2)
    ]
    stores = [
        pltpu.make_async_copy(rows.at[pl.ds(0, 1)], new_weights, sems.at[len(pieces)])
    ]
    stores[0].start()
    for i, (source, scratch, target, row, here) in enumerate(pieces):
        scratch[here, :] = source[here, :] * rows[row : row + 1]
        store = pltpu.make_async_copy(scratch.at[here], target.at[here], sems.at[i])
        store.start()
        stores.append(store)
    for store in stores:
        store.wait()


def on_device(n_cand, n_ref, cand_factor, ref_factor, cand_plan, ref_plan, weights):
    rows_c, depth = cand_factor.shape
    rows_r = ref_factor.shape[0]
    rank = weights.shape[0]
    width_c, width_r = depth // n_ref, depth // n_cand
    part = width_c // 2
    phases = 3 + ITERS
    hbm = pl.BlockSpec(memory_space=pltpu.HBM)
    held = [
        pltpu.with_memory_space_constraint(x, pltpu.HBM)
        for x in (cand_factor, ref_factor, cand_plan, ref_plan, weights.reshape(1, rank))
    ]
    vmem = pl.BlockSpec(memory_space=pltpu.VMEM)
    scaled_cand, scaled_ref, rows_out = pl.pallas_call(
        functools.partial(kernel, n_cand, n_ref),
        out_shape=(
            pltpu.VMEM((rows_c, rank), F32),
            pltpu.VMEM((rows_r, rank), F32),
            pltpu.VMEM((8, rank), F32),
        ),
        in_specs=[hbm] * 5,
        out_specs=(vmem, vmem, vmem),
        scratch_shapes=[
            pltpu.VMEM((depth // LANES, rows_c, LANES), F32),
            pltpu.VMEM((depth // LANES, rows_r, LANES), F32),
            pltpu.VMEM((rows_c, rank), F32),
            pltpu.VMEM((rows_r, rank), F32),
            pltpu.VMEM((1, rank), F32),
            pltpu.VMEM((2, rows_c, depth // 2), BF16),
            pltpu.VMEM((2, rows_c, depth // 2), BF16),
            pltpu.VMEM((2, rows_r, depth // 2), BF16),
            pltpu.VMEM((2, rows_r, depth // 2), BF16),
            pltpu.VMEM((rows_c, rank), F32),
            pltpu.VMEM((rows_r, rank), F32),
            pltpu.VMEM((LANES, rank), F32),
            pltpu.VMEM((LANES, rank), F32),
            pltpu.VMEM((2, part, rank), F32),
            pltpu.VMEM((part, rank), F32),
            pltpu.VMEM((n_cand // 2, part, rank), F32),
            pltpu.VMEM((n_ref, width_r, rank), F32),
            pltpu.VMEM((n_ref, 2, part, rank), F32),
            pltpu.VMEM((depth, rank), F32),
            pltpu.VMEM((1 + ITERS, 2, 1, rank), F32),
            pltpu.VMEM((1 + ITERS, n_cand, 1, rank), F32),
            pltpu.VMEM((1 + ITERS, n_ref, 1, rank), F32),
            pltpu.SemaphoreType.DMA((5,)),
            pltpu.SemaphoreType.DMA((2, depth // LANES)),
            pltpu.SemaphoreType.DMA((3,)),
            pltpu.SemaphoreType.DMA((3,)),
            pltpu.SemaphoreType.DMA((phases,)),
            pltpu.SemaphoreType.DMA((phases,)),
            pltpu.SemaphoreType.DMA((phases,)),
            pltpu.SemaphoreType.DMA((phases,)),
        ],
        compiler_params=pltpu.CompilerParams(
            collective_id=0, has_side_effects=True, vmem_limit_bytes=32 * 2**20
        ),
    )(*held)
    new_cand_plan, new_ref_plan, new_weights = pl.pallas_call(
        finish,
        out_shape=(
            jax.ShapeDtypeStruct((rows_c, rank), F32),
            jax.ShapeDtypeStruct((rows_r, rank), F32),
            jax.ShapeDtypeStruct((1, rank), F32),
        ),
        in_specs=[vmem] * 3,
        out_specs=(hbm, hbm, hbm),
        scratch_shapes=[
            pltpu.VMEM((rows_c, rank), F32),
            pltpu.VMEM((rows_r, rank), F32),
            pltpu.SemaphoreType.DMA((7,)),
        ],
        compiler_params=pltpu.CompilerParams(vmem_limit_bytes=16 * 2**20),
    )(
        *(
            pltpu.with_memory_space_constraint(x, pltpu.VMEM)
            for x in (scaled_cand, scaled_ref, rows_out)
        )
    )
    return new_cand_plan, new_ref_plan, new_weights.reshape(rank)


def solution(mesh):
    in_specs = (P("cand", None), P("ref", None), P("cand", None), P("ref", None), P())
    out_specs = (P("cand", None), P("ref", None), P())
    return jax.shard_map(
        functools.partial(on_device, mesh.shape["cand"], mesh.shape["ref"]),
        mesh=mesh,
        in_specs=in_specs,
        out_specs=out_specs,
        check_vma=False,
    )
```
